128 devices in a mesh: seq: 8 (over z, y_hi), batch: 16 (over y_lo, x, core).
Axes of the slice: x: 4, y: 4 (y_hi: 2, y_lo: 2; y = y_hi * 2 + y_lo), z: 4, core: 2. Of those that a mesh axis runs over, the one named last changes fastest.
Arguments:
- queries: bfloat16 [16, 1536, 2048], P('batch', 'seq'), may hold values from -16 to 16
- key_vectors: bfloat16 [16, 1536, 2048], P('batch', 'seq'), may hold values from -16 to 16
- value_vectors: bfloat16 [16, 1536, 2048], P('batch', 'seq'), may hold values from -6 to 6
- cotangent: bfloat16 [16, 1536, 2048], P('batch', 'seq'), may hold values from -6 to 6
- clip_raw: bfloat16 [2048, 768], P(('seq', 'batch')), may hold values from -0.3984375 to 0.3984375
- text_raw: bfloat16 [2048, 768], P(('seq', 'batch')), may hold values from -0.3984375 to 0.3984375
- clip_video: int32 [2048], P(('seq', 'batch')), may hold values from 0 to 511
- text_video: int32 [2048], P(('seq', 'batch')), may hold values from 0 to 511
- logit_scale: float32 [1], replicated, may hold values from 5 to 15
- logit_bias: float32 [1], replicated, may hold values from -8 to -4
Outputs:
- attended: bfloat16 [16, 1536, 2048], P('batch', 'seq')
- grad_queries: bfloat16 [16, 1536, 2048], P('batch', 'seq')
- grad_keys: bfloat16 [16, 1536, 2048], P('batch', 'seq')
- grad_values: bfloat16 [16, 1536, 2048], P('batch', 'seq')
- grad_clip: float32 [2048, 768], P(('seq', 'batch'))
- grad_text: float32 [2048, 768], P(('seq', 'batch'))
- loss_mean: float32 [1], replicated
The draws below stay inside these ranges and needn't reach their ends.
All inputs are finite; a program needn't handle non-finite values.
Results may differ from the reference program's by a relative error of at most 0.0098.
The reference program's roundings to bfloat16 on the way (of `probs_b`, `dscores` and `pair_grad`) count: a program that leaves them out, or rounds other values in their place, can miss the bound.
Values may be sent and summed in bfloat16 or wider, within the bound.
A program may use at most 64 MiB of HBM per device.

```python
import math
import jax
import jax.numpy as jnp
from jax import lax

HEADS = 16
HD = 128
E = 768
CLIP_DEV = 16
TOKENS = 1536
CLIPS = 16
WIDTH = 2048
NCLIP = 2048
VIDEOS = 512


def draw_queries(key, part):
    key = jax.random.fold_in(key, 1)
    values = jnp.clip(jax.random.normal(key, (CLIPS, TOKENS, WIDTH), jnp.float32), -6.0, 6.0)
    return values.astype(jnp.bfloat16)


def draw_key_vectors(key, part):
    key = jax.random.fold_in(key, 2)
    values = jnp.clip(jax.random.normal(key, (CLIPS, TOKENS, WIDTH), jnp.float32), -6.0, 6.0)
    return values.astype(jnp.bfloat16)


def draw_text_video(key, part):
    key = jax.random.fold_in(key, 3)
    drawn = jax.random.randint(key, (NCLIP,), 0, VIDEOS, jnp.int32)
    ids = drawn * drawn // VIDEOS
    ids = ids.at[0].set(0)
    ids = ids.at[NCLIP - 1].set(VIDEOS - 1)
    return ids.astype(jnp.int32)


def draw_clip_video(key, part):
    key = jax.random.fold_in(key, 4)
    devices = NCLIP // CLIP_DEV
    owner = jnp.arange(NCLIP, dtype=jnp.int32) // CLIP_DEV
    last = max(devices - 1, 1)
    early = last - owner
    low = (VIDEOS // 2 * early + VIDEOS // 64 * owner) // last
    span = (VIDEOS // 2 * early + (VIDEOS // 16 - VIDEOS // 64) * owner) // last
    span = jnp.maximum(span, 1)
    drawn = jax.random.randint(key, (NCLIP,), 0, 1 << 20, jnp.int32)
    ids = low + drawn % span
    ids = ids.at[0].set(VIDEOS - 1)
    ids = ids.at[1].set(0)
    return ids.astype(jnp.int32)


def shard_levels(stream_key, shape, split, least, largest):
    factor_of, own = 1.0, jax.random.fold_in(stream_key, 6)
    for axis_at, parts in split:
        heights = jnp.exp(jax.random.uniform(jax.random.fold_in(own, axis_at), (parts,), jnp.float32, least / len(split), largest / len(split)))
        factor_of = factor_of * jnp.repeat(heights, shape[axis_at] // parts).reshape([-1 if axis == axis_at else 1 for axis in range(len(shape))])
    return factor_of


def scatter_about(rng, shape, width, reach, shards=(), held_as=jnp.bfloat16):
    values = jax.random.normal(rng, shape, jnp.float32) * width
    if len(shards) > 0:
        values = shard_levels(rng, shape, shards, -0.22, 0.18) * values
    return jnp.clip(values, min=-reach, max=reach).astype(held_as)


def setup_inputs(seed: int = 0) -> dict:
    key_list = jax.random.split(jax.random.key(seed), 11)
    return {
        "queries": draw_queries(jax.random.fold_in(key_list[10], 71), 0),
        "key_vectors": draw_key_vectors(jax.random.fold_in(key_list[10], 71), 0),
        "value_vectors": scatter_about(key_list[2], (CLIPS, TOKENS, WIDTH), 1.0, 6.0, ((0, 16), (1, 8))),
        "cotangent": scatter_about(key_list[3], (CLIPS, TOKENS, WIDTH), 1.0, 6.0, ((0, 16), (1, 8))),
        "clip_raw": scatter_about(key_list[4], (NCLIP, E), 0.05, 0.3984375, ((0, 128),)),
        "text_raw": scatter_about(key_list[5], (NCLIP, E), 0.05, 0.3984375, ((0, 128),)),
        "clip_video": draw_clip_video(jax.random.fold_in(key_list[10], 71), 0),
        "text_video": draw_text_video(jax.random.fold_in(key_list[10], 71), 0),
        "logit_scale": jnp.clip(jax.random.uniform(key_list[8], (1,), jnp.float32, 5.0, 15.0), 5.0, 15.0),
        "logit_bias": jnp.clip(jax.random.uniform(key_list[9], (1,), jnp.float32, -8.0, -4.0), -8.0, -4.0),
    }


def attend_head(items):
    q_head, k_head, v_head, d_head = items
    inv_root = 1.0 / math.sqrt(HD)
    hp = lax.Precision.HIGHEST
    qf = q_head.astype(jnp.float32)
    kf = k_head.astype(jnp.float32)
    vf = v_head.astype(jnp.float32)
    df = d_head.astype(jnp.float32)
    scores = jnp.dot(qf, kf.T, precision=hp) * inv_root
    top = lax.optimization_barrier(jnp.max(scores, axis=1, keepdims=True))
    expo = jnp.exp(scores - top)
    probs = expo / lax.optimization_barrier(jnp.sum(expo, axis=1, keepdims=True))
    probs_b = probs.astype(jnp.bfloat16).astype(jnp.float32)
    out_b = jnp.dot(probs_b, vf, precision=hp).astype(jnp.bfloat16)
    grad_v = jnp.dot(probs_b.T, df, precision=hp).astype(jnp.bfloat16)
    dprobs = jnp.dot(df, vf.T, precision=hp)
    delta = lax.optimization_barrier(jnp.sum(df * out_b.astype(jnp.float32), axis=1, keepdims=True))
    dscores = (probs * (dprobs - delta)).astype(jnp.bfloat16).astype(jnp.float32)
    grad_q = (jnp.dot(dscores, kf, precision=hp) * inv_root).astype(jnp.bfloat16)
    grad_k = (jnp.dot(dscores.T, qf, precision=hp) * inv_root).astype(jnp.bfloat16)
    return (out_b, grad_q, grad_k, grad_v)

def to_heads(array):
    return array.reshape(CLIPS, TOKENS, HEADS, HD).transpose(0, 2, 1, 3).reshape(CLIPS * HEADS, TOKENS, HD)

def from_heads(array):
    return array.reshape(CLIPS, HEADS, TOKENS, HD).transpose(0, 2, 1, 3).reshape(CLIPS, TOKENS, WIDTH)

def unit_rows(raw):
    rawf = raw.astype(jnp.float32)
    norm = jnp.sqrt(lax.optimization_barrier(jnp.sum(rawf * rawf, axis=1, keepdims=True)) + 1e-06)
    return (rawf / norm, norm)

def reference(queries, key_vectors, value_vectors, cotangent, clip_raw, text_raw, clip_video, text_video, logit_scale, logit_bias):
    results = lax.map(attend_head, (to_heads(queries), to_heads(key_vectors), to_heads(value_vectors), to_heads(cotangent)))
    attended, grad_queries, grad_keys, grad_values = [from_heads(item) for item in results]
    hp = lax.Precision.HIGHEST
    clip_unit, clip_norm = unit_rows(clip_raw)
    text_unit, text_norm = unit_rows(text_raw)
    clip_b = clip_unit.astype(jnp.bfloat16).astype(jnp.float32)
    text_b = text_unit.astype(jnp.bfloat16).astype(jnp.float32)
    scale = logit_scale[0]
    logits = scale * jnp.dot(clip_b, text_b.T, precision=hp) + logit_bias[0]
    sign = jnp.where(clip_video[:, None] == text_video[None, :], jnp.float32(1.0), jnp.float32(-1.0))
    pair_grad = (scale * -sign * jax.nn.sigmoid(-sign * logits)).astype(jnp.bfloat16).astype(jnp.float32)
    loss_mean = jnp.reshape(jnp.sum(jax.nn.softplus(-sign * logits)) / NCLIP, (1,))
    clip_dir = jnp.dot(pair_grad, text_b, precision=hp)
    text_dir = jnp.dot(pair_grad.T, clip_b, precision=hp)
    grad_clip = (clip_dir - clip_unit * lax.optimization_barrier(jnp.sum(clip_unit * clip_dir, axis=1, keepdims=True))) / clip_norm
    grad_text = (text_dir - text_unit * lax.optimization_barrier(jnp.sum(text_unit * text_dir, axis=1, keepdims=True))) / text_norm
    return (attended, grad_queries, grad_keys, grad_values, grad_clip, grad_text, loss_mean)
```

```python
import functools
import math

import jax
import jax.numpy as jnp
from jax import lax
from jax.experimental import pallas as pl
from jax.experimental.pallas import tpu as pltpu
from jax.sharding import PartitionSpec as P

MESH = pl.DeviceIdType.MESH
F32 = jnp.float32
BF16 = jnp.bfloat16

HD = 128
SEQ = 8
BATCH = 16
NZ = 4
NY = 4
NXC = 8
HEADS_HERE = 2
BLOCK_Q = 512

INV_ROOT = 1.0 / math.sqrt(HD)
EXP2_SCALE = INV_ROOT * math.log2(math.e)


def nt(a, b):
    return lax.dot_general(a, b, (((1,), (1,)), ((), ())), preferred_element_type=F32)


def nn(a, b):
    return lax.dot_general(a, b, (((1,), (0,)), ((), ())), preferred_element_type=F32)


def tn(a, b):
    return lax.dot_general(a, b, (((0,), (0,)), ((), ())), preferred_element_type=F32)


def aligned(index, size):
    return pl.ds(pl.multiple_of(index * size, size), size)


def unit_rows(raw):
    rawf = raw.astype(F32)
    norm = jnp.sqrt(jnp.sum(rawf * rawf, axis=1, keepdims=True) + 1e-06)
    return (rawf / norm, norm)


def raw_grad(raw, direction):
    unit, norm = unit_rows(raw)
    return (direction - unit * jnp.sum(unit * direction, axis=1, keepdims=True)) / norm


def wait_for(ref, sem):
    pltpu.make_async_copy(ref, ref, sem).wait()


def column_of_ids(ids_ref, rows):
    row = lax.broadcasted_iota(jnp.int32, (rows, HD), 0)
    column = jnp.zeros((rows, HD), jnp.int32)
    for i in range(rows):
        column = jnp.where(row == i, ids_ref[i], column)
    return column


def kernel(
    q_in, k_in, v_in, d_in, clip_raw, text_raw, clip_ids, text_ids, scale_ref, bias_ref,
    o_out, dq_out, dk_out, dv_out, grad_clip, grad_text, loss_out,
    land, res, dk_sum, dv_sum,
    clip_y, clip_y_ids, clip_x, clip_x_ids, text_z, text_z_ids,
    dx_send, dx_recv, dy_send, dy_recv, dt_send, dt_recv, loss_send, loss_recv,
    in_send, in_recv, in_local, out_send, out_recv, out_local, small_send, small_recv,
):
    tokens = q_in.shape[1]
    rows = clip_raw.shape[0]
    full = tokens * SEQ
    s = lax.axis_index("seq")
    b = lax.axis_index("batch")
    z, y_hi = s // 2, s % 2
    y_lo, xc = b // NXC, b % NXC
    y = y_hi * 2 + y_lo

    def seq_peer(k):
        return (lax.rem(s + k, SEQ), b)

    def xc_peer(k):
        return (s, y_lo * NXC + lax.rem(xc + k, NXC))

    def y_peer(k):
        other = lax.rem(y + k, NY)
        return (z * 2 + other // 2, (other % 2) * NXC + xc)

    def z_peer(k):
        return (lax.rem(z + k, NZ) * 2 + y_hi, b)

    barrier = pltpu.get_barrier_semaphore()

    def greet(peer):
        pl.semaphore_signal(barrier, inc=1, device_id=peer, device_id_type=MESH)

    for k in range(1, SEQ):
        greet(seq_peer(k))
    for k in range(1, NXC):
        greet(xc_peer(k))
    greet(y_peer(1))
    greet(y_peer(3))

    clip_y[aligned(y, rows), :] = unit_rows(clip_raw[...])[0].astype(BF16)
    text_z[aligned(z, rows), :] = unit_rows(text_raw[...])[0].astype(BF16)
    clip_y_ids[aligned(y, rows), :] = column_of_ids(clip_ids, rows)
    text_z_ids[aligned(z, rows), :] = column_of_ids(text_ids, rows)

    pl.semaphore_wait(barrier, SEQ - 1 + NXC - 1 + 2)

    def send(src, dst, index, peer):
        pltpu.make_async_remote_copy(
            src_ref=src, dst_ref=dst, send_sem=small_send.at[index], recv_sem=small_recv.at[index],
            device_id=peer, device_id_type=MESH,
        ).start()

    for k in range(1, NY):
        mine = aligned(y, rows)
        send(clip_y.at[mine], clip_y.at[mine], 0, y_peer(k))
        send(clip_y_ids.at[mine], clip_y_ids.at[mine], 1, y_peer(k))
    for k in range(1, NZ):
        mine = aligned(z, rows)
        send(text_z.at[mine], text_z.at[mine], 2, z_peer(k))
        send(text_z_ids.at[mine], text_z_ids.at[mine], 3, z_peer(k))

    ins = (k_in, q_in, v_in, d_in)

    def send_head(h):
        for a, ref in enumerate(ins):
            mine = aligned(s, tokens)
            pltpu.make_async_copy(
                ref.at[0, :, aligned(s * HEADS_HERE + h, HD)], land.at[h, a, mine], in_local.at[h, a]
            ).start()

            def to_peer(k, carry):
                peer = seq_peer(k)
                pltpu.make_async_remote_copy(
                    src_ref=ref.at[0, :, aligned(peer[0] * HEADS_HERE + h, HD)],
                    dst_ref=land.at[h, a, mine],
                    send_sem=in_send.at[h, a], recv_sem=in_recv.at[h, a],
                    device_id=peer, device_id_type=MESH,
                ).start()
                return carry

            lax.fori_loop(1, SEQ, to_peer, 0)

    others = full - tokens

    def wait_sent(h):
        for a in range(4):
            wait_for(land.at[h, a, pl.ds(0, others)], in_send.at[h, a])

    def wait_head(h, a):
        wait_for(land.at[h, a, pl.ds(0, others)], in_recv.at[h, a])
        wait_for(land.at[h, a, pl.ds(0, tokens)], in_local.at[h, a])

    send_head(0)

    wait_for(clip_y.at[pl.ds(0, 3 * rows)], small_recv.at[0])
    wait_for(clip_y_ids.at[pl.ds(0, 3 * rows)], small_recv.at[1])
    group = NY * rows
    for k in range(1, NXC):
        send(clip_y, clip_x.at[aligned(xc, group)], 4, xc_peer(k))
        send(clip_y_ids, clip_x_ids.at[aligned(xc, group)], 5, xc_peer(k))
    clip_x[aligned(xc, group), :] = clip_y[...]
    clip_x_ids[aligned(xc, group), :] = clip_y_ids[...]

    wait_sent(0)
    send_head(1)

    wait_for(text_z.at[pl.ds(0, 3 * rows)], small_recv.at[2])
    wait_for(text_z_ids.at[pl.ds(0, 3 * rows)], small_recv.at[3])
    wait_for(clip_x.at[pl.ds(0, 7 * group)], small_recv.at[4])
    wait_for(clip_x_ids.at[pl.ds(0, 7 * group)], small_recv.at[5])
    scale = scale_ref[0]
    offset = bias_ref[0]
    clip_all = clip_x[...]
    text_all = text_z[...]
    texts = NZ * rows
    logits = scale * nt(clip_all, text_all) + offset
    text_row = jnp.transpose(text_z_ids[...].astype(F32))[0:1, :]
    clip_column = clip_x_ids[...].astype(F32)[:, 0:texts]
    sign = jnp.where(clip_column == text_row, F32(1.0), F32(-1.0))
    turned = -sign * logits
    small = jnp.exp(-jnp.abs(turned))
    sigmoid = jnp.where(turned >= 0, F32(1.0), small) / (1.0 + small)
    loss_here = jnp.sum(jnp.maximum(turned, 0.0) + jnp.log1p(small))
    pair_grad = (scale * -sign * sigmoid).astype(BF16)
    text_part = tn(pair_grad, clip_all)
    for j in range(NZ):
        dt_send[j] = text_part[j * rows : (j + 1) * rows]
    clip_part = nn(pair_grad, text_all)
    for j in range(NXC):
        dx_send[j, 0:group] = clip_part[j * group : (j + 1) * group]
        dx_send[j, group : group + 8] = jnp.full((8, clip_part.shape[1]), loss_here, F32)
    for k in range(1, NXC):
        send(dx_send.at[lax.rem(xc + k, NXC)], dx_recv.at[xc], 6, xc_peer(k))
    for k in range(1, NZ):
        send(dt_send.at[lax.rem(z + k, NZ)], dt_recv.at[z], 7, z_peer(k))
    dx_recv[xc] = dx_send[xc]
    dt_recv[z] = dt_send[z]

    def attend(h):
        k_all, q_all, v_all, d_all = (land.at[h, a] for a in range(4))
        for a in range(4):
            wait_head(h, a)
        dk_sum[...] = jnp.zeros_like(dk_sum)
        dv_sum[...] = jnp.zeros_like(dv_sum)

        def step(i, carry):
            r = aligned(i, BLOCK_Q)
            q = q_all[r, :]
            d = d_all[r, :]
            raw_scores = nt(q, k_all[...])
            top = jnp.max(raw_scores, axis=1, keepdims=True)
            expo = jnp.exp2(raw_scores * EXP2_SCALE - top * EXP2_SCALE)
            total = jnp.sum(expo, axis=1, keepdims=True)
            probs = expo * (1.0 / total)
            probs_b = probs.astype(BF16)
            out = nn(probs_b, v_all[...]).astype(BF16)
            res[h, 0, r, :] = out
            dv_sum[...] += tn(probs_b, d)
            dprobs = nt(d, v_all[...])
            delta = jnp.sum(d.astype(F32) * out.astype(F32), axis=1, keepdims=True)
            dscores = (probs * (dprobs - delta)).astype(BF16)
            res[h, 1, r, :] = (nn(dscores, k_all[...]) * INV_ROOT).astype(BF16)
            dk_sum[...] += tn(dscores, q)
            return carry

        lax.fori_loop(0, full // BLOCK_Q, step, 0)
        res[h, 2] = (dk_sum[...] * INV_ROOT).astype(BF16)
        res[h, 3] = dv_sum[...].astype(BF16)

    outs = (o_out, dq_out, dk_out, dv_out)

    def return_head(h):
        for a, ref in enumerate(outs):
            columns = aligned(s * HEADS_HERE + h, HD)
            pltpu.make_async_copy(
                res.at[h, a, aligned(s, tokens)], ref.at[0, :, columns], out_local.at[a]
            ).start()

            def to_peer(k, carry):
                peer = seq_peer(k)
                pltpu.make_async_remote_copy(
                    src_ref=res.at[h, a, aligned(peer[0], tokens)],
                    dst_ref=ref.at[0, :, columns],
                    send_sem=out_send.at[a], recv_sem=out_recv.at[a],
                    device_id=peer, device_id_type=MESH,
                ).start()
                return carry

            lax.fori_loop(1, SEQ, to_peer, 0)

    attend(0)
    return_head(0)

    wait_for(dx_recv.at[pl.ds(0, NXC - 1)], small_recv.at[6])
    clip_sum = dx_recv[0]
    for j in range(1, NXC):
        clip_sum = clip_sum + dx_recv[j]
    for j in range(NY):
        dy_send[j, 0:rows] = clip_sum[j * rows : (j + 1) * rows]
        dy_send[j, rows : rows + 8] = clip_sum[group : group + 8]
    for k in range(1, NY):
        send(dy_send.at[lax.rem(y + k, NY)], dy_recv.at[y], 8, y_peer(k))
    dy_recv[y] = dy_send[y]

    attend(1)
    return_head(1)

    wait_for(dy_recv.at[pl.ds(0, NY - 1)], small_recv.at[8])
    clip_sum = dy_recv[0]
    for j in range(1, NY):
        clip_sum = clip_sum + dy_recv[j]
    loss_send[...] = clip_sum[rows : rows + 8, 0:HD]
    for k in range(1, NZ):
        send(loss_send, loss_recv.at[z], 9, z_peer(k))
    loss_recv[z] = loss_send[...]
    grad_clip[...] = raw_grad(clip_raw[...], clip_sum[0:rows])

    wait_for(dt_recv.at[pl.ds(0, NZ - 1)], small_recv.at[7])
    text_sum = dt_recv[0]
    for j in range(1, NZ):
        text_sum = text_sum + dt_recv[j]
    grad_text[...] = raw_grad(text_raw[...], text_sum)

    wait_for(loss_recv.at[pl.ds(0, NZ - 1)], small_recv.at[9])
    loss_sum = loss_recv[0]
    for j in range(1, NZ):
        loss_sum = loss_sum + loss_recv[j]
    loss_out[0] = loss_sum[0, 0] / (rows * SEQ * BATCH)

    for index, ref in (
        (0, clip_y.at[pl.ds(0, 3 * rows)]),
        (1, clip_y_ids.at[pl.ds(0, 3 * rows)]),
        (2, text_z.at[pl.ds(0, 3 * rows)]),
        (3, text_z_ids.at[pl.ds(0, 3 * rows)]),
        (4, clip_x.at[pl.ds(0, 7 * group)]),
        (5, clip_x_ids.at[pl.ds(0, 7 * group)]),
        (6, dx_recv.at[pl.ds(0, NXC - 1)]),
        (7, dt_recv.at[pl.ds(0, NZ - 1)]),
        (8, dy_recv.at[pl.ds(0, NY - 1)]),
        (9, loss_recv.at[pl.ds(0, NZ - 1)]),
    ):
        wait_for(ref, small_send.at[index])
    wait_sent(1)
    remote = HEADS_HERE * (SEQ - 1) * HD
    for a, ref in enumerate(outs):
        wait_for(ref.at[0, :, pl.ds(0, HEADS_HERE * HD)], out_local.at[a])
        wait_for(ref.at[0, :, pl.ds(0, remote)], out_send.at[a])
        wait_for(ref.at[0, :, pl.ds(0, remote)], out_recv.at[a])


def body(queries, key_vectors, value_vectors, cotangent, clip_raw, text_raw, clip_video, text_video, logit_scale, logit_bias):
    tokens = queries.shape[1]
    full = tokens * SEQ
    rows, width = clip_raw.shape
    in_hbm = pl.BlockSpec(memory_space=pl.ANY)
    in_vmem = pl.BlockSpec(memory_space=pltpu.VMEM)
    in_smem = pl.BlockSpec(memory_space=pltpu.SMEM)
    group = NY * rows
    dma = pltpu.SemaphoreType.DMA
    return pl.pallas_call(
        kernel,
        out_shape=(
            *[jax.ShapeDtypeStruct(queries.shape, BF16)] * 4,
            jax.ShapeDtypeStruct((rows, width), F32),
            jax.ShapeDtypeStruct((rows, width), F32),
            jax.ShapeDtypeStruct((1,), F32),
        ),
        in_specs=[in_hbm] * 4 + [in_vmem] * 2 + [in_smem] * 4,
        out_specs=(*[in_hbm] * 4, in_vmem, in_vmem, in_smem),
        scratch_shapes=[
            pltpu.VMEM((HEADS_HERE, 4, full, HD), BF16),
            pltpu.VMEM((HEADS_HERE, 4, full, HD), BF16),
            pltpu.VMEM((full, HD), F32),
            pltpu.VMEM((full, HD), F32),
            pltpu.VMEM((group, width), BF16),
            pltpu.VMEM((group, HD), jnp.int32),
            pltpu.VMEM((NXC * group, width), BF16),
            pltpu.VMEM((NXC * group, HD), jnp.int32),
            pltpu.VMEM((NZ * rows, width), BF16),
            pltpu.VMEM((NZ * rows, HD), jnp.int32),
            pltpu.VMEM((NXC, group + 8, width), F32),
            pltpu.VMEM((NXC, group + 8, width), F32),
            pltpu.VMEM((NY, rows + 8, width), F32),
            pltpu.VMEM((NY, rows + 8, width), F32),
            pltpu.VMEM((NZ, rows, width), F32),
            pltpu.VMEM((NZ, rows, width), F32),
            pltpu.VMEM((8, HD), F32),
            pltpu.VMEM((NZ, 8, HD), F32),
            dma((HEADS_HERE, 4)),
            dma((HEADS_HERE, 4)),
            dma((HEADS_HERE, 4)),
            dma((4,)),
            dma((4,)),
            dma((4,)),
            dma((10,)),
            dma((10,)),
        ],
        compiler_params=pltpu.CompilerParams(
            collective_id=0, has_side_effects=True, vmem_limit_bytes=56 * 2**20
        ),
        cost_estimate=pl.CostEstimate(
            flops=HEADS_HERE * 12 * full * full * HD, bytes_accessed=8 * full * HD * 2, transcendentals=HEADS_HERE * full * full
        ),
        name="tower",
    )(queries, key_vectors, value_vectors, cotangent, clip_raw, text_raw, clip_video, text_video, logit_scale, logit_bias)


def solution(mesh):
    tokens = P("batch", "seq", None)
    embeddings = P(("seq", "batch"), None)
    ids = P(("seq", "batch"))
    return jax.shard_map(
        body,
        mesh=mesh,
        in_specs=(tokens,) * 4 + (embeddings,) * 2 + (ids,) * 2 + (P(), P()),
        out_specs=(tokens,) * 4 + (embeddings,) * 2 + (P(),),
        check_vma=False,
    )
```

```python
import functools
import math

import jax
import jax.numpy as jnp
from jax import lax
from jax.experimental import pallas as pl
from jax.experimental.pallas import tpu as pltpu
from jax.sharding import PartitionSpec as P

MESH = pl.DeviceIdType.MESH
F32 = jnp.float32
BF16 = jnp.bfloat16

HD = 128
SEQ = 8
BATCH = 16
NZ = 4
NY = 4
NX = 4
NC = 2
HEADS_HERE = 2
BLOCK_Q = 512
PIECES = 2

INV_ROOT = 1.0 / math.sqrt(HD)
EXP2_SCALE = INV_ROOT * math.log2(math.e)


def nt(a, b):
    return lax.dot_general(a, b, (((1,), (1,)), ((), ())), preferred_element_type=F32)


def nn(a, b):
    return lax.dot_general(a, b, (((1,), (0,)), ((), ())), preferred_element_type=F32)


def tn(a, b):
    return lax.dot_general(a, b, (((0,), (0,)), ((), ())), preferred_element_type=F32)


def aligned(index, size):
    return pl.ds(pl.multiple_of(index * size, size), size)


def unit_rows(raw):
    rawf = raw.astype(F32)
    norm = jnp.sqrt(jnp.sum(rawf * rawf, axis=1, keepdims=True) + 1e-06)
    return (rawf / norm, norm)


def raw_grad(raw, direction):
    unit, norm = unit_rows(raw)
    return (direction - unit * jnp.sum(unit * direction, axis=1, keepdims=True)) / norm


def wait_for(ref, sem):
    pltpu.make_async_copy(ref, ref, sem).wait()


def column_of_ids(ids_ref, rows):
    row = lax.broadcasted_iota(jnp.int32, (rows, HD), 0)
    column = jnp.zeros((rows, HD), jnp.int32)
    for i in range(rows):
        column = jnp.where(row == i, ids_ref[i], column)
    return column


def kernel(
    q_in, k_in, v_in, d_in, clip_raw, text_raw, clip_ids, text_ids, scale_ref, bias_ref,
    o_out, dq_out, dk_out, dv_out, grad_clip, grad_text, loss_out,
    land, res, dk_sum, dv_sum,
    clip_y, clip_y_ids, clip_x, clip_x_ids, text_z, text_z_ids, text_c, text_c_ids,
    dc_send, dc_recv, dx_send, dx_recv, near_send, near_recv, far_send, far_recv, loss_y, dt_send, dt_recv, loss_send, loss_recv,
    in_send, in_recv, in_local, out_send, out_recv, out_local, small_send, small_recv,
):
    tokens = q_in.shape[1]
    rows = clip_raw.shape[0]
    full = tokens * SEQ
    s = lax.axis_index("seq")
    b = lax.axis_index("batch")
    z, y_hi = s // 2, s % 2
    y_lo, x, c = b // (NX * NC), (b // NC) % NX, b % NC
    y = y_hi * 2 + y_lo

    def seq_peer(k):
        return (lax.rem(s + k, SEQ), b)

    def x_peer(k):
        return (s, (y_lo * NX + lax.rem(x + k, NX)) * NC + c)

    def y_peer(k):
        other = lax.rem(y + k, NY)
        return (z * 2 + other // 2, ((other % 2) * NX + x) * NC + c)

    y_near = (s, b + (1 - 2 * y_lo) * NX * NC)
    y_far = (s + 1 - 2 * y_hi, b)
    c_peer = (s, b + 1 - 2 * c)

    def z_peer(k):
        return (lax.rem(z + k, NZ) * 2 + y_hi, b)

    barrier = pltpu.get_barrier_semaphore()

    def greet(peer):
        pl.semaphore_signal(barrier, inc=1, device_id=peer, device_id_type=MESH)

    for k in range(1, SEQ):
        greet(seq_peer(k))
    for k in range(1, NX):
        greet(x_peer(k))
    greet(c_peer)
    greet(y_peer(1))
    greet(y_peer(3))

    clip_y[aligned(y, rows), :] = unit_rows(clip_raw[...])[0].astype(BF16)
    text_z[aligned(z, rows), :] = unit_rows(text_raw[...])[0].astype(BF16)
    clip_y_ids[aligned(y, rows), :] = column_of_ids(clip_ids, rows)
    text_z_ids[aligned(z, rows), :] = column_of_ids(text_ids, rows)

    pl.semaphore_wait(barrier, SEQ - 1 + NX - 1 + 3)

    def send(src, dst, index, peer):
        pltpu.make_async_remote_copy(
            src_ref=src, dst_ref=dst, send_sem=small_send.at[index], recv_sem=small_recv.at[index],
            device_id=peer, device_id_type=MESH,
        ).start()

    for k in range(1, NY):
        mine = aligned(y, rows)
        send(clip_y.at[mine], clip_y.at[mine], 0, y_peer(k))
        send(clip_y_ids.at[mine], clip_y_ids.at[mine], 1, y_peer(k))
    for k in range(1, NZ):
        mine = aligned(z, rows)
        send(text_z.at[mine], text_z.at[mine], 2, z_peer(k))
        send(text_z_ids.at[mine], text_z_ids.at[mine], 3, z_peer(k))

    ins = (k_in, q_in, v_in, d_in)

    def send_head(h):
        for a, ref in enumerate(ins):
            mine = aligned(s, tokens)
            pltpu.make_async_copy(
                ref.at[0, :, aligned(s * HEADS_HERE + h, HD)], land.at[h, a, mine], in_local.at[h, a]
            ).start()

            def to_peer(k, carry):
                peer = seq_peer(k)
                pltpu.make_async_remote_copy(
                    src_ref=ref.at[0, :, aligned(peer[0] * HEADS_HERE + h, HD)],
                    dst_ref=land.at[h, a, mine],
                    send_sem=in_send.at[h, a], recv_sem=in_recv.at[h, a],
                    device_id=peer, device_id_type=MESH,
                ).start()
                return carry

            lax.fori_loop(1, SEQ, to_peer, 0)

    others = full - tokens

    def wait_sent(h):
        for a in range(4):
            wait_for(land.at[h, a, pl.ds(0, others)], in_send.at[h, a])

    def wait_head(h, a):
        wait_for(land.at[h, a, pl.ds(0, others)], in_recv.at[h, a])
        wait_for(land.at[h, a, pl.ds(0, tokens)], in_local.at[h, a])

    wait_for(clip_y.at[pl.ds(0, 3 * rows)], small_recv.at[0])
    wait_for(clip_y_ids.at[pl.ds(0, 3 * rows)], small_recv.at[1])
    wait_for(text_z.at[pl.ds(0, 3 * rows)], small_recv.at[2])
    wait_for(text_z_ids.at[pl.ds(0, 3 * rows)], small_recv.at[3])

    send_head(0)

    group = NY * rows
    for k in range(1, NX):
        send(clip_y, clip_x.at[aligned(x, group)], 4, x_peer(k))
        send(clip_y_ids, clip_x_ids.at[aligned(x, group)], 5, x_peer(k))
    clip_x[aligned(x, group), :] = clip_y[...]
    clip_x_ids[aligned(x, group), :] = clip_y_ids[...]
    send(text_z, text_c.at[aligned(c, group)], 6, c_peer)
    send(text_z_ids, text_c_ids.at[aligned(c, group)], 7, c_peer)
    text_c[aligned(c, group), :] = text_z[...]
    text_c_ids[aligned(c, group), :] = text_z_ids[...]

    wait_for(text_c.at[pl.ds(0, group)], small_recv.at[6])
    wait_for(text_c_ids.at[pl.ds(0, group)], small_recv.at[7])
    wait_for(clip_x.at[pl.ds(0, 3 * group)], small_recv.at[4])
    wait_for(clip_x_ids.at[pl.ds(0, 3 * group)], small_recv.at[5])
    scale = scale_ref[0]
    offset = bias_ref[0]
    clip_all = clip_x[...]
    text_all = text_c[...]
    logits = scale * nt(clip_all, text_all) + offset
    text_row = jnp.transpose(text_c_ids[...].astype(F32))[0:1, :]
    sign = jnp.where(clip_x_ids[...].astype(F32) == text_row, F32(1.0), F32(-1.0))
    turned = -sign * logits
    small = jnp.exp(-jnp.abs(turned))
    sigmoid = jnp.where(turned >= 0, F32(1.0), small) / (1.0 + small)
    loss_here = jnp.sum(jnp.maximum(turned, 0.0) + jnp.log1p(small))
    pair_grad = (scale * -sign * sigmoid).astype(BF16)
    text_part = tn(pair_grad, clip_all)
    for j in range(NC):
        dc_send[j, 0:group] = text_part[j * group : (j + 1) * group]
        dc_send[j, group : group + 8] = jnp.full((8, text_part.shape[1]), loss_here, F32)
    send(dc_send.at[1 - c], dc_recv, 8, c_peer)
    clip_part = nn(pair_grad, text_all)
    for j in range(NX):
        dx_send[j, 0:group] = clip_part[j * group : (j + 1) * group]
    wait_for(dc_recv, small_recv.at[8])
    text_sum = dc_send[c] + dc_recv[...]
    for j in range(NZ):
        dt_send[j] = text_sum[j * rows : (j + 1) * rows]
    for j in range(NX):
        dx_send[j, group : group + 8] = text_sum[group : group + 8]
    for k in range(1, NX):
        send(dx_send.at[lax.rem(x + k, NX)], dx_recv.at[x], 9, x_peer(k))
    for k in range(1, NZ):
        send(dt_send.at[lax.rem(z + k, NZ)], dt_recv.at[z], 10, z_peer(k))
    dx_recv[x] = dx_send[x]
    dt_recv[z] = dt_send[z]

    wait_sent(0)
    send_head(1)

    def attend(h):
        k_all, q_all, v_all, d_all = (land.at[h, a] for a in range(4))
        for a in range(4):
            wait_head(h, a)
        dk_sum[...] = jnp.zeros_like(dk_sum)
        dv_sum[...] = jnp.zeros_like(dv_sum)

        def step(i, carry):
            r = aligned(i, BLOCK_Q)
            q = q_all[r, :]
            d = d_all[r, :]
            raw_scores = nt(q, k_all[...])
            top = jnp.max(raw_scores, axis=1, keepdims=True)
            expo = jnp.exp2(raw_scores * EXP2_SCALE - top * EXP2_SCALE)
            total = jnp.sum(expo, axis=1, keepdims=True)
            probs = expo * (1.0 / total)
            probs_b = probs.astype(BF16)
            out = nn(probs_b, v_all[...]).astype(BF16)
            res[h, 0, r, :] = out
            dv_sum[...] += tn(probs_b, d)
            dprobs = nt(d, v_all[...])
            delta = jnp.sum(d.astype(F32) * out.astype(F32), axis=1, keepdims=True)
            dscores = (probs * (dprobs - delta)).astype(BF16)
            res[h, 1, r, :] = (nn(dscores, k_all[...]) * INV_ROOT).astype(BF16)
            dk_sum[...] += tn(dscores, q)
            return carry

        lax.fori_loop(0, full // BLOCK_Q, step, 0)
        res[h, 2] = (dk_sum[...] * INV_ROOT).astype(BF16)
        res[h, 3] = dv_sum[...].astype(BF16)

    outs = (o_out, dq_out, dk_out, dv_out)

    def return_head(h):
        for a, ref in enumerate(outs):
            columns = aligned(s * HEADS_HERE + h, HD)
            pltpu.make_async_copy(
                res.at[h, a, aligned(s, tokens)], ref.at[0, :, columns], out_local.at[a]
            ).start()

            def to_peer(k, carry):
                peer = seq_peer(k)
                pltpu.make_async_remote_copy(
                    src_ref=res.at[h, a, aligned(peer[0], tokens)],
                    dst_ref=ref.at[0, :, columns],
                    send_sem=out_send.at[a], recv_sem=out_recv.at[a],
                    device_id=peer, device_id_type=MESH,
                ).start()
                return carry

            lax.fori_loop(1, SEQ, to_peer, 0)

    attend(0)
    return_head(0)

    wait_for(dx_recv.at[pl.ds(0, NX - 1)], small_recv.at[9])
    clip_sum = dx_recv[0]
    for j in range(1, NX):
        clip_sum = clip_sum + dx_recv[j]
    for j in range(2):
        near_send[j, 0:rows] = clip_sum[j * rows : (j + 1) * rows]
        near_send[j, rows : 2 * rows] = clip_sum[(2 + j) * rows : (3 + j) * rows]
    loss_y[0] = clip_sum[group : group + 8, 0:HD]
    send(near_send.at[1 - y_lo], near_recv, 11, y_near)
    send(loss_y.at[0], loss_y.at[1], 13, y_near)

    attend(1)

    wait_for(near_recv, small_recv.at[11])
    wait_for(loss_y.at[0], small_recv.at[13])
    clip_sum = near_send[y_lo] + near_recv[...]
    for j in range(2):
        far_send[j] = clip_sum[j * rows : (j + 1) * rows]
    loss_y[2] = loss_y[0] + loss_y[1]
    send(far_send.at[1 - y_hi], far_recv, 14, y_far)
    send(loss_y.at[2], loss_y.at[3], 15, y_far)

    return_head(1)

    wait_for(far_recv, small_recv.at[14])
    wait_for(loss_y.at[0], small_recv.at[15])
    clip_sum = far_send[y_hi] + far_recv[...]
    loss_send[...] = loss_y[2] + loss_y[3]
    for k in range(1, NZ):
        send(loss_send, loss_recv.at[z], 12, z_peer(k))
    loss_recv[z] = loss_send[...]
    grad_clip[...] = raw_grad(clip_raw[...], clip_sum)

    wait_for(dt_recv.at[pl.ds(0, NZ - 1)], small_recv.at[10])
    text_sum = dt_recv[0]
    for j in range(1, NZ):
        text_sum = text_sum + dt_recv[j]
    grad_text[...] = raw_grad(text_raw[...], text_sum)

    wait_for(loss_recv.at[pl.ds(0, NZ - 1)], small_recv.at[12])
    loss_sum = loss_recv[0]
    for j in range(1, NZ):
        loss_sum = loss_sum + loss_recv[j]
    loss_out[...] = loss_sum / (rows * SEQ * BATCH)

    for index, ref in (
        (0, clip_y.at[pl.ds(0, 3 * rows)]),
        (1, clip_y_ids.at[pl.ds(0, 3 * rows)]),
        (2, text_z.at[pl.ds(0, 3 * rows)]),
        (3, text_z_ids.at[pl.ds(0, 3 * rows)]),
        (4, clip_x.at[pl.ds(0, 3 * group)]),
        (5, clip_x_ids.at[pl.ds(0, 3 * group)]),
        (6, text_c.at[pl.ds(0, group)]),
        (7, text_c_ids.at[pl.ds(0, group)]),
        (8, dc_recv),
        (9, dx_recv.at[pl.ds(0, NX - 1)]),
        (10, dt_recv.at[pl.ds(0, NZ - 1)]),
        (11, near_recv),
        (13, loss_y.at[0]),
        (14, far_recv),
        (15, loss_y.at[0]),
        (12, loss_recv.at[pl.ds(0, NZ - 1)]),
    ):
        wait_for(ref, small_send.at[index])
    wait_sent(1)
    remote = HEADS_HERE * (SEQ - 1) * HD
    for a, ref in enumerate(outs):
        wait_for(ref.at[0, :, pl.ds(0, HEADS_HERE * HD)], out_local.at[a])
        wait_for(ref.at[0, :, pl.ds(0, remote)], out_send.at[a])
        wait_for(ref.at[0, :, pl.ds(0, remote)], out_recv.at[a])


def hand_over(*refs):
    sources, targets, (held, held_grad, held_loss, load, store) = refs[:7], refs[7:14], refs[14:]
    size = held.shape[1] // PIECES
    loads, stores = [], []

    def through(source, middle, target):
        index = len(loads)
        loads.append(pltpu.make_async_copy(source, middle, load.at[index]))
        stores.append(pltpu.make_async_copy(middle, target, store.at[index]))

    for a in range(4):
        for i in range(PIECES):
            part = pl.ds(i * size, size)
            through(sources[a].at[0, part], held.at[a, part], targets[a].at[0, part])
    for a in range(2):
        through(sources[4 + a], held_grad.at[a], targets[4 + a])
    loss = pltpu.make_async_copy(sources[6], held_loss, load.at[len(loads)])
    for copy in loads:
        copy.start()
    loss.start()
    for arrived, copy in zip(loads, stores):
        arrived.wait()
        copy.start()
    loss.wait()
    targets[6][0] = held_loss[0, 0]
    for copy in stores:
        copy.wait()


def body(queries, key_vectors, value_vectors, cotangent, clip_raw, text_raw, clip_video, text_video, logit_scale, logit_bias):
    tokens = queries.shape[1]
    full = tokens * SEQ
    rows, width = clip_raw.shape
    in_hbm = pl.BlockSpec(memory_space=pl.ANY)
    in_vmem = pl.BlockSpec(memory_space=pltpu.VMEM)
    in_smem = pl.BlockSpec(memory_space=pltpu.SMEM)
    group = NY * rows
    dma = pltpu.SemaphoreType.DMA
    results = pl.pallas_call(
        kernel,
        out_shape=(
            *[jax.ShapeDtypeStruct(queries.shape, BF16)] * 4,
            jax.ShapeDtypeStruct((rows, width), F32),
            jax.ShapeDtypeStruct((rows, width), F32),
            jax.ShapeDtypeStruct((8, HD), F32),
        ),
        in_specs=[in_hbm] * 4 + [in_vmem] * 2 + [in_smem] * 4,
        out_specs=(*[in_hbm] * 4, in_vmem, in_vmem, in_vmem),
        scratch_shapes=[
            pltpu.VMEM((HEADS_HERE, 4, full, HD), BF16),
            pltpu.VMEM((HEADS_HERE, 4, full, HD), BF16),
            pltpu.VMEM((full, HD), F32),
            pltpu.VMEM((full, HD), F32),
            pltpu.VMEM((group, width), BF16),
            pltpu.VMEM((group, HD), jnp.int32),
            pltpu.VMEM((NX * group, width), BF16),
            pltpu.VMEM((NX * group, HD), jnp.int32),
            pltpu.VMEM((NZ * rows, width), BF16),
            pltpu.VMEM((NZ * rows, HD), jnp.int32),
            pltpu.VMEM((NC * NZ * rows, width), BF16),
            pltpu.VMEM((NC * NZ * rows, HD), jnp.int32),
            pltpu.VMEM((NC, group + 8, width), F32),
            pltpu.VMEM((group + 8, width), F32),
            pltpu.VMEM((NX, group + 8, width), F32),
            pltpu.VMEM((NX, group + 8, width), F32),
            pltpu.VMEM((2, 2 * rows, width), F32),
            pltpu.VMEM((2 * rows, width), F32),
            pltpu.VMEM((2, rows, width), F32),
            pltpu.VMEM((rows, width), F32),
            pltpu.VMEM((4, 8, HD), F32),
            pltpu.VMEM((NZ, rows, width), F32),
            pltpu.VMEM((NZ, rows, width), F32),
            pltpu.VMEM((8, HD), F32),
            pltpu.VMEM((NZ, 8, HD), F32),
            dma((HEADS_HERE, 4)),
            dma((HEADS_HERE, 4)),
            dma((HEADS_HERE, 4)),
            dma((4,)),
            dma((4,)),
            dma((4,)),
            dma((16,)),
            dma((16,)),
        ],
        compiler_params=pltpu.CompilerParams(
            collective_id=0, has_side_effects=True, vmem_limit_bytes=56 * 2**20
        ),
        cost_estimate=pl.CostEstimate(
            flops=HEADS_HERE * 12 * full * full * HD, bytes_accessed=8 * full * HD * 2, transcendentals=HEADS_HERE * full * full
        ),
        name="tower",
    )(queries, key_vectors, value_vectors, cotangent, clip_raw, text_raw, clip_video, text_video, logit_scale, logit_bias)
    return pl.pallas_call(
        hand_over,
        out_shape=(
            *[jax.ShapeDtypeStruct(queries.shape, BF16)] * 4,
            jax.ShapeDtypeStruct((rows, width), F32),
            jax.ShapeDtypeStruct((rows, width), F32),
            jax.ShapeDtypeStruct((1,), F32),
        ),
        in_specs=[in_hbm] * 7,
        out_specs=(*[in_hbm] * 6, in_smem),
        scratch_shapes=[
            pltpu.VMEM((4, tokens, queries.shape[2]), BF16),
            pltpu.VMEM((2, rows, width), F32),
            pltpu.VMEM((8, HD), F32),
            dma((4 * PIECES + 3,)),
            dma((4 * PIECES + 2,)),
        ],
        name="hand_over",
    )(*results)


def solution(mesh):
    tokens = P("batch", "seq", None)
    embeddings = P(("seq", "batch"), None)
    ids = P(("seq", "batch"))
    return jax.shard_map(
        body,
        mesh=mesh,
        in_specs=(tokens,) * 4 + (embeddings,) * 2 + (ids,) * 2 + (P(), P()),
        out_specs=(tokens,) * 4 + (embeddings,) * 2 + (P(),),
        check_vma=False,
    )
```

```python
import functools
import math

import jax
import jax.numpy as jnp
from jax import lax
from jax.experimental import pallas as pl
from jax.experimental.pallas import tpu as pltpu
from jax.sharding import PartitionSpec as P

MESH = pl.DeviceIdType.MESH
F32 = jnp.float32
BF16 = jnp.bfloat16

HD = 128
SEQ = 8
BATCH = 16
NZ = 4
NY = 4
NX = 4
NC = 2
HEADS_HERE = 2
BLOCK_Q = 512

INV_ROOT = 1.0 / math.sqrt(HD)
EXP2_SCALE = INV_ROOT * math.log2(math.e)


def nt(a, b):
    return lax.dot_general(a, b, (((1,), (1,)), ((), ())), preferred_element_type=F32)


def nn(a, b):
    return lax.dot_general(a, b, (((1,), (0,)), ((), ())), preferred_element_type=F32)


def tn(a, b):
    return lax.dot_general(a, b, (((0,), (0,)), ((), ())), preferred_element_type=F32)


def aligned(index, size):
    return pl.ds(pl.multiple_of(index * size, size), size)


def unit_rows(raw):
    rawf = raw.astype(F32)
    norm = jnp.sqrt(jnp.sum(rawf * rawf, axis=1, keepdims=True) + 1e-06)
    return (rawf / norm, norm)


def raw_grad(raw, direction):
    unit, norm = unit_rows(raw)
    return (direction - unit * jnp.sum(unit * direction, axis=1, keepdims=True)) / norm


def wait_for(ref, sem):
    pltpu.make_async_copy(ref, ref, sem).wait()


def column_of_ids(ids_ref, rows):
    row = lax.broadcasted_iota(jnp.int32, (rows, HD), 0)
    column = jnp.zeros((rows, HD), jnp.int32)
    for i in range(rows):
        column = jnp.where(row == i, ids_ref[i], column)
    return column


def kernel(
    q_in, k_in, v_in, d_in, clip_in, text_in, clip_ids_in, text_ids_in, scale_ref, bias_ref,
    o_out, dq_out, dk_out, dv_out, grad_clip, grad_text, loss_out,
    clip_ids, text_ids, load, land, res, dk_sum, dv_sum,
    clip_y, clip_y_ids, clip_x, clip_x_ids, text_z, text_z_ids, text_c, text_c_ids,
    dc_send, dc_recv, dx_send, dx_recv, near_send, near_recv, far_send, far_recv, loss_y, dt_send, dt_recv, loss_recv,
    in_send, in_recv, in_local, out_send, out_recv, out_local, small_send, small_recv,
):
    tokens = q_in.shape[1]
    rows = clip_in.shape[0]
    scalars = [
        pltpu.make_async_copy(clip_ids_in, clip_ids, load.at[2]),
        pltpu.make_async_copy(text_ids_in, text_ids, load.at[3]),
    ]
    for copy in scalars:
        copy.start()
    full = tokens * SEQ
    s = lax.axis_index("seq")
    b = lax.axis_index("batch")
    z, y_hi = s // 2, s % 2
    y_lo, x, c = b // (NX * NC), (b // NC) % NX, b % NC
    y = y_hi * 2 + y_lo

    def seq_peer(k):
        return (lax.rem(s + k, SEQ), b)

    def x_peer(k):
        return (s, (y_lo * NX + lax.rem(x + k, NX)) * NC + c)

    def y_peer(k):
        other = lax.rem(y + k, NY)
        return (z * 2 + other // 2, ((other % 2) * NX + x) * NC + c)

    y_near = (s, b + (1 - 2 * y_lo) * NX * NC)
    y_far = (s + 1 - 2 * y_hi, b)
    c_peer = (s, b + 1 - 2 * c)

    def z_peer(k):
        return (lax.rem(z + k, NZ) * 2 + y_hi, b)

    barrier = pltpu.get_barrier_semaphore()

    def greet(peer):
        pl.semaphore_signal(barrier, inc=1, device_id=peer, device_id_type=MESH)

    for k in range(1, SEQ):
        greet(seq_peer(k))
    for k in range(1, NX):
        greet(x_peer(k))
    greet(c_peer)
    greet(y_peer(1))
    greet(y_peer(3))

    for copy in scalars:
        copy.wait()
    clip_y_ids[aligned(y, rows), :] = column_of_ids(clip_ids, rows)
    text_z_ids[aligned(z, rows), :] = column_of_ids(text_ids, rows)
    clip_own = aligned(y, rows)
    text_own = aligned(z, rows)
    clip_load = pltpu.make_async_copy(clip_in, clip_y.at[clip_own], load.at[0])
    text_load = pltpu.make_async_copy(text_in, text_z.at[text_own], load.at[1])
    clip_load.start()
    text_load.start()

    pl.semaphore_wait(barrier, SEQ - 1 + NX - 1 + 3)

    def send(src, dst, index, peer):
        pltpu.make_async_remote_copy(
            src_ref=src, dst_ref=dst, send_sem=small_send.at[index], recv_sem=small_recv.at[index],
            device_id=peer, device_id_type=MESH,
        ).start()

    for k in range(1, NY):
        send(clip_in, clip_y.at[clip_own], 0, y_peer(k))
        send(clip_y_ids.at[clip_own], clip_y_ids.at[clip_own], 1, y_peer(k))
    for k in range(1, NZ):
        send(text_in, text_z.at[text_own], 2, z_peer(k))
        send(text_z_ids.at[text_own], text_z_ids.at[text_own], 3, z_peer(k))

    ins = (k_in, q_in, v_in, d_in)

    def send_head(h):
        for a, ref in enumerate(ins):
            mine = aligned(s, tokens)
            pltpu.make_async_copy(
                ref.at[0, :, aligned(s * HEADS_HERE + h, HD)], land.at[h, a, mine], in_local.at[h, a]
            ).start()

            def to_peer(k, carry):
                peer = seq_peer(k)
                pltpu.make_async_remote_copy(
                    src_ref=ref.at[0, :, aligned(peer[0] * HEADS_HERE + h, HD)],
                    dst_ref=land.at[h, a, mine],
                    send_sem=in_send.at[h, a], recv_sem=in_recv.at[h, a],
                    device_id=peer, device_id_type=MESH,
                ).start()
                return carry

            lax.fori_loop(1, SEQ, to_peer, 0)

    others = full - tokens

    def wait_sent(h):
        for a in range(4):
            wait_for(land.at[h, a, pl.ds(0, others)], in_send.at[h, a])

    def wait_head(h, a):
        wait_for(land.at[h, a, pl.ds(0, others)], in_recv.at[h, a])
        wait_for(land.at[h, a, pl.ds(0, tokens)], in_local.at[h, a])

    wait_for(clip_y.at[pl.ds(0, 3 * rows)], small_recv.at[0])
    wait_for(clip_y_ids.at[pl.ds(0, 3 * rows)], small_recv.at[1])
    wait_for(text_z.at[pl.ds(0, 3 * rows)], small_recv.at[2])
    wait_for(text_z_ids.at[pl.ds(0, 3 * rows)], small_recv.at[3])

    send_head(0)

    group = NY * rows
    clip_load.wait()
    text_load.wait()
    for k in range(1, NX):
        send(clip_y, clip_x.at[aligned(x, group)], 4, x_peer(k))
        send(clip_y_ids, clip_x_ids.at[aligned(x, group)], 5, x_peer(k))
    clip_x[aligned(x, group), :] = clip_y[...]
    clip_x_ids[aligned(x, group), :] = clip_y_ids[...]
    send(text_z, text_c.at[aligned(c, group)], 6, c_peer)
    send(text_z_ids, text_c_ids.at[aligned(c, group)], 7, c_peer)
    text_c[aligned(c, group), :] = text_z[...]
    text_c_ids[aligned(c, group), :] = text_z_ids[...]

    wait_for(text_c.at[pl.ds(0, group)], small_recv.at[6])
    wait_for(text_c_ids.at[pl.ds(0, group)], small_recv.at[7])
    wait_for(clip_x.at[pl.ds(0, 3 * group)], small_recv.at[4])
    wait_for(clip_x_ids.at[pl.ds(0, 3 * group)], small_recv.at[5])
    scale = scale_ref[0]
    offset = bias_ref[0]
    clip_all = unit_rows(clip_x[...])[0].astype(BF16)
    text_all = unit_rows(text_c[...])[0].astype(BF16)
    logits = scale * nt(clip_all, text_all) + offset
    text_row = jnp.transpose(text_c_ids[...].astype(F32))[0:1, :]
    sign = jnp.where(clip_x_ids[...].astype(F32) == text_row, F32(1.0), F32(-1.0))
    turned = -sign * logits
    small = jnp.exp(-jnp.abs(turned))
    sigmoid = jnp.where(turned >= 0, F32(1.0), small) / (1.0 + small)
    loss_here = jnp.sum(jnp.maximum(turned, 0.0) + jnp.log1p(small))
    pair_grad = (scale * -sign * sigmoid).astype(BF16)
    text_part = tn(pair_grad, clip_all)
    for j in range(NC):
        dc_send[j, 0:group] = text_part[j * group : (j + 1) * group]
        dc_send[j, group : group + 8] = jnp.full((8, text_part.shape[1]), loss_here, F32)
    send(dc_send.at[1 - c], dc_recv, 8, c_peer)
    clip_part = nn(pair_grad, text_all)
    for j in range(NX):
        dx_send[j, 0:group] = clip_part[j * group : (j + 1) * group]
    wait_for(dc_recv, small_recv.at[8])
    text_sum = dc_send[c] + dc_recv[...]
    for j in range(NZ):
        dt_send[j] = text_sum[j * rows : (j + 1) * rows]
    for j in range(NX):
        dx_send[j, group : group + 8] = text_sum[group : group + 8]
    for k in range(1, NX):
        send(dx_send.at[lax.rem(x + k, NX)], dx_recv.at[x], 9, x_peer(k))
    for k in range(1, NZ):
        send(dt_send.at[lax.rem(z + k, NZ)], dt_recv.at[z], 10, z_peer(k))
    dx_recv[x] = dx_send[x]
    dt_recv[z] = dt_send[z]

    wait_sent(0)
    send_head(1)

    def attend(h):
        k_all, q_all, v_all, d_all = (land.at[h, a] for a in range(4))
        for a in range(4):
            wait_head(h, a)
        dk_sum[...] = jnp.zeros_like(dk_sum)
        dv_sum[...] = jnp.zeros_like(dv_sum)

        def step(i, carry):
            r = aligned(i, BLOCK_Q)
            q = q_all[r, :]
            d = d_all[r, :]
            raw_scores = nt(q, k_all[...])
            top = jnp.max(raw_scores, axis=1, keepdims=True)
            expo = jnp.exp2(raw_scores * EXP2_SCALE - top * EXP2_SCALE)
            total = jnp.sum(expo, axis=1, keepdims=True)
            probs = expo * (1.0 / total)
            probs_b = probs.astype(BF16)
            out = nn(probs_b, v_all[...]).astype(BF16)
            res[h, 0, r, :] = out
            dv_sum[...] += tn(probs_b, d)
            dprobs = nt(d, v_all[...])
            delta = jnp.sum(d.astype(F32) * out.astype(F32), axis=1, keepdims=True)
            dscores = (probs * (dprobs - delta)).astype(BF16)
            res[h, 1, r, :] = (nn(dscores, k_all[...]) * INV_ROOT).astype(BF16)
            dk_sum[...] += tn(dscores, q)
            return carry

        lax.fori_loop(0, full // BLOCK_Q, step, 0)
        res[h, 2] = (dk_sum[...] * INV_ROOT).astype(BF16)
        res[h, 3] = dv_sum[...].astype(BF16)

    outs = (o_out, dq_out, dk_out, dv_out)

    def return_head(h):
        for a, ref in enumerate(outs):
            columns = aligned(s * HEADS_HERE + h, HD)
            pltpu.make_async_copy(
                res.at[h, a, aligned(s, tokens)], ref.at[0, :, columns], out_local.at[a]
            ).start()

            def to_peer(k, carry):
                peer = seq_peer(k)
                pltpu.make_async_remote_copy(
                    src_ref=res.at[h, a, aligned(peer[0], tokens)],
                    dst_ref=ref.at[0, :, columns],
                    send_sem=out_send.at[a], recv_sem=out_recv.at[a],
                    device_id=peer, device_id_type=MESH,
                ).start()
                return carry

            lax.fori_loop(1, SEQ, to_peer, 0)

    attend(0)
    return_head(0)

    wait_for(dx_recv.at[pl.ds(0, NX - 1)], small_recv.at[9])
    clip_sum = dx_recv[0]
    for j in range(1, NX):
        clip_sum = clip_sum + dx_recv[j]
    for j in range(2):
        near_send[j, 0:rows] = clip_sum[j * rows : (j + 1) * rows]
        near_send[j, rows : 2 * rows] = clip_sum[(2 + j) * rows : (3 + j) * rows]
    loss_y[0] = clip_sum[group : group + 8, 0:HD]
    send(near_send.at[1 - y_lo], near_recv, 11, y_near)
    send(loss_y.at[0], loss_y.at[1], 13, y_near)

    attend(1)

    wait_for(near_recv, small_recv.at[11])
    wait_for(loss_y.at[0], small_recv.at[13])
    clip_sum = near_send[y_lo] + near_recv[...]
    for j in range(2):
        far_send[j] = clip_sum[j * rows : (j + 1) * rows]
    loss_recv[s] = loss_y[0] + loss_y[1]
    send(far_send.at[1 - y_hi], far_recv, 14, y_far)
    for k in range(1, SEQ):
        send(loss_recv.at[s], loss_recv.at[s], 12, seq_peer(k))

    return_head(1)

    wait_for(far_recv, small_recv.at[14])
    clip_sum = far_send[y_hi] + far_recv[...]
    grad_clip[...] = raw_grad(clip_y[clip_own, :], clip_sum)

    wait_for(dt_recv.at[pl.ds(0, NZ - 1)], small_recv.at[10])
    text_sum = dt_recv[0]
    for j in range(1, NZ):
        text_sum = text_sum + dt_recv[j]
    grad_text[...] = raw_grad(text_z[text_own, :], text_sum)

    wait_for(loss_recv.at[pl.ds(0, SEQ - 1)], small_recv.at[12])
    loss_sum = loss_recv[0]
    for j in range(1, SEQ):
        loss_sum = loss_sum + loss_recv[j]
    loss_out[...] = loss_sum / (rows * SEQ * BATCH)

    for index, ref in (
        (0, clip_y.at[pl.ds(0, 3 * rows)]),
        (1, clip_y_ids.at[pl.ds(0, 3 * rows)]),
        (2, text_z.at[pl.ds(0, 3 * rows)]),
        (3, text_z_ids.at[pl.ds(0, 3 * rows)]),
        (4, clip_x.at[pl.ds(0, 3 * group)]),
        (5, clip_x_ids.at[pl.ds(0, 3 * group)]),
        (6, text_c.at[pl.ds(0, group)]),
        (7, text_c_ids.at[pl.ds(0, group)]),
        (8, dc_recv),
        (9, dx_recv.at[pl.ds(0, NX - 1)]),
        (10, dt_recv.at[pl.ds(0, NZ - 1)]),
        (11, near_recv),
        (13, loss_y.at[0]),
        (14, far_recv),
        (12, loss_recv.at[pl.ds(0, SEQ - 1)]),
    ):
        wait_for(ref, small_send.at[index])
    wait_sent(1)
    remote = HEADS_HERE * (SEQ - 1) * HD
    for a, ref in enumerate(outs):
        wait_for(ref.at[0, :, pl.ds(0, HEADS_HERE * HD)], out_local.at[a])
        wait_for(ref.at[0, :, pl.ds(0, remote)], out_send.at[a])
        wait_for(ref.at[0, :, pl.ds(0, remote)], out_recv.at[a])


def hand_over(*refs):
    sources, targets, sems = refs[:7], refs[7:14], refs[14]
    copies = [pltpu.make_async_copy(sources[a], targets[a], sems.at[a]) for a in range(6)]
    for copy in copies:
        copy.start()
    targets[6][0] = sources[6][0, 0]
    for copy in copies:
        copy.wait()


def body(queries, key_vectors, value_vectors, cotangent, clip_raw, text_raw, clip_video, text_video, logit_scale, logit_bias):
    tokens = queries.shape[1]
    full = tokens * SEQ
    rows, width = clip_raw.shape
    in_hbm = pl.BlockSpec(memory_space=pl.ANY)
    in_vmem = pl.BlockSpec(memory_space=pltpu.VMEM)
    in_smem = pl.BlockSpec(memory_space=pltpu.SMEM)
    group = NY * rows
    dma = pltpu.SemaphoreType.DMA
    in_place = (queries, key_vectors, value_vectors, cotangent, clip_raw, text_raw, clip_video, text_video)
    results = pl.pallas_call(
        kernel,
        out_shape=(
            *[pltpu.VMEM(queries.shape, BF16)] * 4,
            pltpu.VMEM((rows, width), F32),
            pltpu.VMEM((rows, width), F32),
            pltpu.VMEM((8, HD), F32),
        ),
        in_specs=[in_hbm] * 8 + [in_smem] * 2,
        out_specs=[in_vmem] * 7,
        scratch_shapes=[
            pltpu.SMEM((rows,), jnp.int32),
            pltpu.SMEM((rows,), jnp.int32),
            dma((4,)),
            pltpu.VMEM((HEADS_HERE, 4, full, HD), BF16),
            pltpu.VMEM((HEADS_HERE, 4, full, HD), BF16),
            pltpu.VMEM((full, HD), F32),
            pltpu.VMEM((full, HD), F32),
            pltpu.VMEM((group, width), BF16),
            pltpu.VMEM((group, HD), jnp.int32),
            pltpu.VMEM((NX * group, width), BF16),
            pltpu.VMEM((NX * group, HD), jnp.int32),
            pltpu.VMEM((NZ * rows, width), BF16),
            pltpu.VMEM((NZ * rows, HD), jnp.int32),
            pltpu.VMEM((NC * NZ * rows, width), BF16),
            pltpu.VMEM((NC * NZ * rows, HD), jnp.int32),
            pltpu.VMEM((NC, group + 8, width), F32),
            pltpu.VMEM((group + 8, width), F32),
            pltpu.VMEM((NX, group + 8, width), F32),
            pltpu.VMEM((NX, group + 8, width), F32),
            pltpu.VMEM((2, 2 * rows, width), F32),
            pltpu.VMEM((2 * rows, width), F32),
            pltpu.VMEM((2, rows, width), F32),
            pltpu.VMEM((rows, width), F32),
            pltpu.VMEM((2, 8, HD), F32),
            pltpu.VMEM((NZ, rows, width), F32),
            pltpu.VMEM((NZ, rows, width), F32),
            pltpu.VMEM((SEQ, 8, HD), F32),
            dma((HEADS_HERE, 4)),
            dma((HEADS_HERE, 4)),
            dma((HEADS_HERE, 4)),
            dma((4,)),
            dma((4,)),
            dma((4,)),
            dma((15,)),
            dma((15,)),
        ],
        compiler_params=pltpu.CompilerParams(
            collective_id=0, has_side_effects=True, vmem_limit_bytes=48 * 2**20
        ),
        cost_estimate=pl.CostEstimate(
            flops=HEADS_HERE * 12 * full * full * HD, bytes_accessed=8 * full * HD * 2, transcendentals=HEADS_HERE * full * full
        ),
        name="tower",
    )(*[pltpu.with_memory_space_constraint(array, pltpu.HBM) for array in in_place], logit_scale, logit_bias)
    return pl.pallas_call(
        hand_over,
        out_shape=(
            *[jax.ShapeDtypeStruct(queries.shape, BF16)] * 4,
            jax.ShapeDtypeStruct((rows, width), F32),
            jax.ShapeDtypeStruct((rows, width), F32),
            jax.ShapeDtypeStruct((1,), F32),
        ),
        in_specs=[in_vmem] * 7,
        out_specs=(*[in_hbm] * 6, in_smem),
        scratch_shapes=[dma((6,))],
        name="hand_over",
    )(*[pltpu.with_memory_space_constraint(array, pltpu.VMEM) for array in results])


def solution(mesh):
    tokens = P("batch", "seq", None)
    embeddings = P(("seq", "batch"), None)
    ids = P(("seq", "batch"))
    return jax.shard_map(
        body,
        mesh=mesh,
        in_specs=(tokens,) * 4 + (embeddings,) * 2 + (ids,) * 2 + (P(), P()),
        out_specs=(tokens,) * 4 + (embeddings,) * 2 + (P(),),
        check_vma=False,
    )
```

```python
import functools
import math

import jax
import jax.numpy as jnp
from jax import lax
from jax.experimental import pallas as pl
from jax.experimental.pallas import tpu as pltpu
from jax.sharding import PartitionSpec as P

MESH = pl.DeviceIdType.MESH
F32 = jnp.float32
BF16 = jnp.bfloat16

HD = 128
SEQ = 8
BATCH = 16
NZ = 4
NY = 4
NX = 4
NC = 2
HEADS_HERE = 2
BLOCK_Q = 512

INV_ROOT = 1.0 / math.sqrt(HD)
EXP2_SCALE = INV_ROOT * math.log2(math.e)


def nt(a, b):
    return lax.dot_general(a, b, (((1,), (1,)), ((), ())), preferred_element_type=F32)


def nn(a, b):
    return lax.dot_general(a, b, (((1,), (0,)), ((), ())), preferred_element_type=F32)


def tn(a, b):
    return lax.dot_general(a, b, (((0,), (0,)), ((), ())), preferred_element_type=F32)


def aligned(index, size):
    return pl.ds(pl.multiple_of(index * size, size), size)


def unit_rows(raw):
    rawf = raw.astype(F32)
    norm = jnp.sqrt(jnp.sum(rawf * rawf, axis=1, keepdims=True) + 1e-06)
    return (rawf / norm, norm)


def across(unit, direction):
    return direction - unit * jnp.sum(unit * direction, axis=1, keepdims=True)


def raw_grad(raw, direction):
    unit, norm = unit_rows(raw)
    return across(unit, direction) / norm


def wait_for(ref, sem):
    pltpu.make_async_copy(ref, ref, sem).wait()


def column_of_ids(ids_ref, rows):
    row = lax.broadcasted_iota(jnp.int32, (rows, HD), 0)
    column = jnp.zeros((rows, HD), jnp.int32)
    for i in range(rows):
        column = jnp.where(row == i, ids_ref[i], column)
    return column


def kernel(
    q_in, k_in, v_in, d_in, clip_in, text_in, clip_ids_in, text_ids_in, scale_ref, bias_ref,
    o_out, dq_out, dk_out, dv_out, grad_clip, grad_text, loss_out,
    clip_ids, text_ids, load, land, res, dk_sum, dv_sum,
    clip_y, clip_y_ids, clip_x, clip_x_ids, text_z, text_z_ids, text_c, text_c_ids,
    dc_send, dc_recv, dx_send, dx_recv, near_own, near_send, near_recv, far_own, far_send, far_recv, loss_y, dt_own, dt_send, dt_recv, loss_recv,
    in_send, in_recv, in_local, out_send, out_recv, out_local, small_send, small_recv,
):
    tokens = q_in.shape[1]
    rows = clip_in.shape[0]
    scalars = [
        pltpu.make_async_copy(clip_ids_in, clip_ids, load.at[2]),
        pltpu.make_async_copy(text_ids_in, text_ids, load.at[3]),
    ]
    for copy in scalars:
        copy.start()
    full = tokens * SEQ
    s = lax.axis_index("seq")
    b = lax.axis_index("batch")
    z, y_hi = s // 2, s % 2
    y_lo, x, c = b // (NX * NC), (b // NC) % NX, b % NC
    y = y_hi * 2 + y_lo

    def seq_peer(k):
        return (lax.rem(s + k, SEQ), b)

    def x_peer(k):
        return (s, (y_lo * NX + lax.rem(x + k, NX)) * NC + c)

    def y_peer(k):
        other = lax.rem(y + k, NY)
        return (z * 2 + other // 2, ((other % 2) * NX + x) * NC + c)

    y_near = (s, b + (1 - 2 * y_lo) * NX * NC)
    y_far = (s + 1 - 2 * y_hi, b)
    c_peer = (s, b + 1 - 2 * c)

    def z_peer(k):
        return (lax.rem(z + k, NZ) * 2 + y_hi, b)

    barrier = pltpu.get_barrier_semaphore()

    def greet(peer):
        pl.semaphore_signal(barrier, inc=1, device_id=peer, device_id_type=MESH)

    for k in range(1, SEQ):
        greet(seq_peer(k))
    for k in range(1, NX):
        greet(x_peer(k))
    greet(c_peer)
    greet(y_peer(1))
    greet(y_peer(3))

    for copy in scalars:
        copy.wait()
    clip_y_ids[aligned(y, rows), :] = column_of_ids(clip_ids, rows)
    text_z_ids[aligned(z, rows), :] = column_of_ids(text_ids, rows)
    clip_own = aligned(y, rows)
    text_own = aligned(z, rows)
    clip_load = pltpu.make_async_copy(clip_in, clip_y.at[clip_own], load.at[0])
    text_load = pltpu.make_async_copy(text_in, text_z.at[text_own], load.at[1])
    clip_load.start()
    text_load.start()

    pl.semaphore_wait(barrier, SEQ - 1 + NX - 1 + 3)

    def send(src, dst, index, peer):
        pltpu.make_async_remote_copy(
            src_ref=src, dst_ref=dst, send_sem=small_send.at[index], recv_sem=small_recv.at[index],
            device_id=peer, device_id_type=MESH,
        ).start()

    for k in range(1, NY):
        send(clip_in, clip_y.at[clip_own], 0, y_peer(k))
        send(clip_y_ids.at[clip_own], clip_y_ids.at[clip_own], 1, y_peer(k))
    for k in range(1, NZ):
        send(text_in, text_z.at[text_own], 2, z_peer(k))
        send(text_z_ids.at[text_own], text_z_ids.at[text_own], 3, z_peer(k))

    ins = (k_in, q_in, v_in, d_in)

    def send_head(h):
        for a, ref in enumerate(ins):
            mine = aligned(s, tokens)
            pltpu.make_async_copy(
                ref.at[0, :, aligned(s * HEADS_HERE + h, HD)], land.at[h, a, mine], in_local.at[h, a]
            ).start()

            def to_peer(k, carry):
                peer = seq_peer(k)
                pltpu.make_async_remote_copy(
                    src_ref=ref.at[0, :, aligned(peer[0] * HEADS_HERE + h, HD)],
                    dst_ref=land.at[h, a, mine],
                    send_sem=in_send.at[h, a], recv_sem=in_recv.at[h, a],
                    device_id=peer, device_id_type=MESH,
                ).start()
                return carry

            lax.fori_loop(1, SEQ, to_peer, 0)

    others = full - tokens

    def wait_sent(h):
        for a in range(4):
            wait_for(land.at[h, a, pl.ds(0, others)], in_send.at[h, a])

    def wait_head(h, a):
        wait_for(land.at[h, a, pl.ds(0, others)], in_recv.at[h, a])
        wait_for(land.at[h, a, pl.ds(0, tokens)], in_local.at[h, a])

    wait_for(clip_y.at[pl.ds(0, 3 * rows)], small_recv.at[0])
    wait_for(clip_y_ids.at[pl.ds(0, 3 * rows)], small_recv.at[1])
    wait_for(text_z.at[pl.ds(0, 3 * rows)], small_recv.at[2])
    wait_for(text_z_ids.at[pl.ds(0, 3 * rows)], small_recv.at[3])

    send_head(0)

    group = NY * rows
    clip_load.wait()
    text_load.wait()
    for k in range(1, NX):
        send(clip_y, clip_x.at[aligned(x, group)], 4, x_peer(k))
        send(clip_y_ids, clip_x_ids.at[aligned(x, group)], 5, x_peer(k))
    clip_x[aligned(x, group), :] = clip_y[...]
    clip_x_ids[aligned(x, group), :] = clip_y_ids[...]
    send(text_z, text_c.at[aligned(c, group)], 6, c_peer)
    send(text_z_ids, text_c_ids.at[aligned(c, group)], 7, c_peer)
    text_c[aligned(c, group), :] = text_z[...]
    text_c_ids[aligned(c, group), :] = text_z_ids[...]

    wait_for(text_c.at[pl.ds(0, group)], small_recv.at[6])
    wait_for(text_c_ids.at[pl.ds(0, group)], small_recv.at[7])
    wait_for(clip_x.at[pl.ds(0, 3 * group)], small_recv.at[4])
    wait_for(clip_x_ids.at[pl.ds(0, 3 * group)], small_recv.at[5])
    scale = scale_ref[0]
    offset = bias_ref[0]
    clip_all = unit_rows(clip_x[...])[0].astype(BF16)
    text_all = unit_rows(text_c[...])[0].astype(BF16)
    logits = scale * nt(clip_all, text_all) + offset
    text_row = jnp.transpose(text_c_ids[...].astype(F32))[0:1, :]
    sign = jnp.where(clip_x_ids[...].astype(F32) == text_row, F32(1.0), F32(-1.0))
    turned = -sign * logits
    small = jnp.exp(-jnp.abs(turned))
    sigmoid = jnp.where(turned >= 0, F32(1.0), small) / (1.0 + small)
    loss_here = jnp.sum(jnp.maximum(turned, 0.0) + jnp.log1p(small))
    pair_grad = (scale * -sign * sigmoid).astype(BF16)
    text_part = tn(pair_grad, clip_all)
    for j in range(NC):
        dc_send[j, 0:group] = text_part[j * group : (j + 1) * group]
        dc_send[j, group : group + 8] = jnp.full((8, text_part.shape[1]), loss_here, F32)
    send(dc_send.at[1 - c], dc_recv, 8, c_peer)
    clip_part = nn(pair_grad, text_all)
    for j in range(NX):
        dx_send[j, 0:group] = clip_part[j * group : (j + 1) * group]
    wait_for(dc_recv, small_recv.at[8])
    text_sum = dc_send[c] + dc_recv[...]
    text_across = across(unit_rows(text_z[...])[0], text_sum[0:group])
    for j in range(NZ):
        dt_own[j] = text_across[j * rows : (j + 1) * rows]
        dt_send[j] = dt_own[j].astype(BF16)
    for j in range(NX):
        dx_send[j, group : group + 8] = text_sum[group : group + 8]
    for k in range(1, NX):
        send(dx_send.at[lax.rem(x + k, NX)], dx_recv.at[x], 9, x_peer(k))
    for k in range(1, NZ):
        send(dt_send.at[lax.rem(z + k, NZ)], dt_recv.at[z], 10, z_peer(k))
    dx_recv[x] = dx_send[x]
    dt_recv[z] = jnp.zeros(dt_recv.shape[1:], BF16)

    wait_sent(0)
    send_head(1)

    def attend(h):
        k_all, q_all, v_all, d_all = (land.at[h, a] for a in range(4))
        for a in range(4):
            wait_head(h, a)
        dk_sum[...] = jnp.zeros_like(dk_sum)
        dv_sum[...] = jnp.zeros_like(dv_sum)

        def step(i, carry):
            r = aligned(i, BLOCK_Q)
            q = q_all[r, :]
            d = d_all[r, :]
            raw_scores = nt(q, k_all[...])
            top = jnp.max(raw_scores, axis=1, keepdims=True)
            expo = jnp.exp2(raw_scores * EXP2_SCALE - top * EXP2_SCALE)
            total = jnp.sum(expo, axis=1, keepdims=True)
            probs = expo * (1.0 / total)
            probs_b = probs.astype(BF16)
            out = nn(probs_b, v_all[...]).astype(BF16)
            res[h, 0, r, :] = out
            dv_sum[...] += tn(probs_b, d)
            dprobs = nt(d, v_all[...])
            delta = jnp.sum(d.astype(F32) * out.astype(F32), axis=1, keepdims=True)
            dscores = (probs * (dprobs - delta)).astype(BF16)
            res[h, 1, r, :] = (nn(dscores, k_all[...]) * INV_ROOT).astype(BF16)
            dk_sum[...] += tn(dscores, q)
            return carry

        lax.fori_loop(0, full // BLOCK_Q, step, 0)
        res[h, 2] = (dk_sum[...] * INV_ROOT).astype(BF16)
        res[h, 3] = dv_sum[...].astype(BF16)

    outs = (o_out, dq_out, dk_out, dv_out)

    def return_head(h):
        for a, ref in enumerate(outs):
            columns = aligned(s * HEADS_HERE + h, HD)
            pltpu.make_async_copy(
                res.at[h, a, aligned(s, tokens)], ref.at[0, :, columns], out_local.at[a]
            ).start()

            def to_peer(k, carry):
                peer = seq_peer(k)
                pltpu.make_async_remote_copy(
                    src_ref=res.at[h, a, aligned(peer[0], tokens)],
                    dst_ref=ref.at[0, :, columns],
                    send_sem=out_send.at[a], recv_sem=out_recv.at[a],
                    device_id=peer, device_id_type=MESH,
                ).start()
                return carry

            lax.fori_loop(1, SEQ, to_peer, 0)

    attend(0)
    return_head(0)

    wait_for(dx_recv.at[pl.ds(0, NX - 1)], small_recv.at[9])
    clip_sum = dx_recv[0]
    for j in range(1, NX):
        clip_sum = clip_sum + dx_recv[j]
    clip_across = across(unit_rows(clip_y[...])[0], clip_sum[0:group])
    for j in range(2):
        near_own[j, 0:rows] = clip_across[j * rows : (j + 1) * rows]
        near_own[j, rows : 2 * rows] = clip_across[(2 + j) * rows : (3 + j) * rows]
        near_send[j] = near_own[j].astype(BF16)
    loss_y[0] = clip_sum[group : group + 8, 0:HD]
    send(near_send.at[1 - y_lo], near_recv, 11, y_near)
    send(loss_y.at[0], loss_y.at[1], 13, y_near)

    attend(1)

    wait_for(near_recv, small_recv.at[11])
    wait_for(loss_y.at[0], small_recv.at[13])
    clip_sum = near_own[y_lo] + near_recv[...].astype(F32)
    for j in range(2):
        far_own[j] = clip_sum[j * rows : (j + 1) * rows]
        far_send[j] = far_own[j].astype(BF16)
    loss_recv[s] = loss_y[0] + loss_y[1]
    send(far_send.at[1 - y_hi], far_recv, 14, y_far)
    for k in range(1, SEQ):
        send(loss_recv.at[s], loss_recv.at[s], 12, seq_peer(k))

    return_head(1)

    wait_for(far_recv, small_recv.at[14])
    clip_sum = far_own[y_hi] + far_recv[...].astype(F32)
    grad_clip[...] = raw_grad(clip_y[clip_own, :], clip_sum)

    wait_for(dt_recv.at[pl.ds(0, NZ - 1)], small_recv.at[10])
    text_sum = dt_own[z]
    for j in range(NZ):
        text_sum = text_sum + dt_recv[j].astype(F32)
    grad_text[...] = raw_grad(text_z[text_own, :], text_sum)

    wait_for(loss_recv.at[pl.ds(0, SEQ - 1)], small_recv.at[12])
    loss_sum = loss_recv[0]
    for j in range(1, SEQ):
        loss_sum = loss_sum + loss_recv[j]
    loss_out[...] = loss_sum / (rows * SEQ * BATCH)

    for index, ref in (
        (0, clip_y.at[pl.ds(0, 3 * rows)]),
        (1, clip_y_ids.at[pl.ds(0, 3 * rows)]),
        (2, text_z.at[pl.ds(0, 3 * rows)]),
        (3, text_z_ids.at[pl.ds(0, 3 * rows)]),
        (4, clip_x.at[pl.ds(0, 3 * group)]),
        (5, clip_x_ids.at[pl.ds(0, 3 * group)]),
        (6, text_c.at[pl.ds(0, group)]),
        (7, text_c_ids.at[pl.ds(0, group)]),
        (8, dc_recv),
        (9, dx_recv.at[pl.ds(0, NX - 1)]),
        (10, dt_recv.at[pl.ds(0, NZ - 1)]),
        (11, near_recv),
        (13, loss_y.at[0]),
        (14, far_recv),
        (12, loss_recv.at[pl.ds(0, SEQ - 1)]),
    ):
        wait_for(ref, small_send.at[index])
    wait_sent(1)
    remote = HEADS_HERE * (SEQ - 1) * HD
    for a, ref in enumerate(outs):
        wait_for(ref.at[0, :, pl.ds(0, HEADS_HERE * HD)], out_local.at[a])
        wait_for(ref.at[0, :, pl.ds(0, remote)], out_send.at[a])
        wait_for(ref.at[0, :, pl.ds(0, remote)], out_recv.at[a])


def hand_over(*refs):
    sources, targets, sems = refs[:7], refs[7:14], refs[14]
    copies = [pltpu.make_async_copy(sources[a], targets[a], sems.at[a]) for a in range(6)]
    for copy in copies:
        copy.start()
    targets[6][0] = sources[6][0, 0]
    for copy in copies:
        copy.wait()


def body(queries, key_vectors, value_vectors, cotangent, clip_raw, text_raw, clip_video, text_video, logit_scale, logit_bias):
    tokens = queries.shape[1]
    full = tokens * SEQ
    rows, width = clip_raw.shape
    in_hbm = pl.BlockSpec(memory_space=pl.ANY)
    in_vmem = pl.BlockSpec(memory_space=pltpu.VMEM)
    in_smem = pl.BlockSpec(memory_space=pltpu.SMEM)
    group = NY * rows
    dma = pltpu.SemaphoreType.DMA
    in_place = (queries, key_vectors, value_vectors, cotangent, clip_raw, text_raw, clip_video, text_video)
    results = pl.pallas_call(
        kernel,
        out_shape=(
            *[pltpu.VMEM(queries.shape, BF16)] * 4,
            pltpu.VMEM((rows, width), F32),
            pltpu.VMEM((rows, width), F32),
            pltpu.VMEM((8, HD), F32),
        ),
        in_specs=[in_hbm] * 8 + [in_smem] * 2,
        out_specs=[in_vmem] * 7,
        scratch_shapes=[
            pltpu.SMEM((rows,), jnp.int32),
            pltpu.SMEM((rows,), jnp.int32),
            dma((4,)),
            pltpu.VMEM((HEADS_HERE, 4, full, HD), BF16),
            pltpu.VMEM((HEADS_HERE, 4, full, HD), BF16),
            pltpu.VMEM((full, HD), F32),
            pltpu.VMEM((full, HD), F32),
            pltpu.VMEM((group, width), BF16),
            pltpu.VMEM((group, HD), jnp.int32),
            pltpu.VMEM((NX * group, width), BF16),
            pltpu.VMEM((NX * group, HD), jnp.int32),
            pltpu.VMEM((NZ * rows, width), BF16),
            pltpu.VMEM((NZ * rows, HD), jnp.int32),
            pltpu.VMEM((NC * NZ * rows, width), BF16),
            pltpu.VMEM((NC * NZ * rows, HD), jnp.int32),
            pltpu.VMEM((NC, group + 8, width), F32),
            pltpu.VMEM((group + 8, width), F32),
            pltpu.VMEM((NX, group + 8, width), F32),
            pltpu.VMEM((NX, group + 8, width), F32),
            pltpu.VMEM((2, 2 * rows, width), F32),
            pltpu.VMEM((2, 2 * rows, width), BF16),
            pltpu.VMEM((2 * rows, width), BF16),
            pltpu.VMEM((2, rows, width), F32),
            pltpu.VMEM((2, rows, width), BF16),
            pltpu.VMEM((rows, width), BF16),
            pltpu.VMEM((2, 8, HD), F32),
            pltpu.VMEM((NZ, rows, width), F32),
            pltpu.VMEM((NZ, rows, width), BF16),
            pltpu.VMEM((NZ, rows, width), BF16),
            pltpu.VMEM((SEQ, 8, HD), F32),
            dma((HEADS_HERE, 4)),
            dma((HEADS_HERE, 4)),
            dma((HEADS_HERE, 4)),
            dma((4,)),
            dma((4,)),
            dma((4,)),
            dma((15,)),
            dma((15,)),
        ],
        compiler_params=pltpu.CompilerParams(
            collective_id=0, has_side_effects=True, vmem_limit_bytes=48 * 2**20
        ),
        cost_estimate=pl.CostEstimate(
            flops=HEADS_HERE * 12 * full * full * HD, bytes_accessed=8 * full * HD * 2, transcendentals=HEADS_HERE * full * full
        ),
        name="tower",
    )(*[pltpu.with_memory_space_constraint(array, pltpu.HBM) for array in in_place], logit_scale, logit_bias)
    return pl.pallas_call(
        hand_over,
        out_shape=(
            *[jax.ShapeDtypeStruct(queries.shape, BF16)] * 4,
            jax.ShapeDtypeStruct((rows, width), F32),
            jax.ShapeDtypeStruct((rows, width), F32),
            jax.ShapeDtypeStruct((1,), F32),
        ),
        in_specs=[in_vmem] * 7,
        out_specs=(*[in_hbm] * 6, in_smem),
        scratch_shapes=[dma((6,))],
        name="hand_over",
    )(*[pltpu.with_memory_space_constraint(array, pltpu.VMEM) for array in results])


def solution(mesh):
    tokens = P("batch", "seq", None)
    embeddings = P(("seq", "batch"), None)
    ids = P(("seq", "batch"))
    return jax.shard_map(
        body,
        mesh=mesh,
        in_specs=(tokens,) * 4 + (embeddings,) * 2 + (ids,) * 2 + (P(), P()),
        out_specs=(tokens,) * 4 + (embeddings,) * 2 + (P(),),
        check_vma=False,
    )
```

```python
import functools
import math

import jax
import jax.numpy as jnp
from jax import lax
from jax.experimental import pallas as pl
from jax.experimental.pallas import tpu as pltpu
from jax.sharding import PartitionSpec as P

MESH = pl.DeviceIdType.MESH
F32 = jnp.float32
BF16 = jnp.bfloat16

HD = 128
SEQ = 8
BATCH = 16
NZ = 4
NY = 4
NX = 4
NC = 2
HEADS_HERE = 2
BLOCK_Q = 512

INV_ROOT = 1.0 / math.sqrt(HD)
EXP2_SCALE = INV_ROOT * math.log2(math.e)


def nt(a, b):
    return lax.dot_general(a, b, (((1,), (1,)), ((), ())), preferred_element_type=F32)


def nn(a, b):
    return lax.dot_general(a, b, (((1,), (0,)), ((), ())), preferred_element_type=F32)


def tn(a, b):
    return lax.dot_general(a, b, (((0,), (0,)), ((), ())), preferred_element_type=F32)


def aligned(index, size):
    return pl.ds(pl.multiple_of(index * size, size), size)


def unit_rows(raw):
    rawf = raw.astype(F32)
    norm = jnp.sqrt(jnp.sum(rawf * rawf, axis=1, keepdims=True) + 1e-06)
    return (rawf / norm, norm)


def across(unit, direction):
    return direction - unit * jnp.sum(unit * direction, axis=1, keepdims=True)


def raw_grad(raw, direction):
    unit, norm = unit_rows(raw)
    return across(unit, direction) / norm


def wait_for(ref, sem):
    pltpu.make_async_copy(ref, ref, sem).wait()


def column_of_ids(ids_ref, rows):
    row = lax.broadcasted_iota(jnp.int32, (rows, HD), 0)
    column = jnp.zeros((rows, HD), jnp.int32)
    for i in range(rows):
        column = jnp.where(row == i, ids_ref[i], column)
    return column


def kernel(
    q_in, k_in, v_in, d_in, clip_in, text_in, clip_ids_in, text_ids_in, scale_ref, bias_ref,
    o_out, dq_out, dk_out, dv_out, grad_clip, grad_text, loss_out,
    clip_ids, text_ids, load, land, res, dk_sum, dv_sum,
    clip_y, clip_y_ids, clip_x, clip_x_ids, text_z, text_z_ids, text_c, text_c_ids,
    dc_send, dc_recv, dx_send, dx_recv, near_own, near_send, near_recv, far_own, far_send, far_recv, loss_y, dt_own, dt_send, dt_recv, loss_recv,
    in_send, in_recv, in_local, out_send, out_recv, out_local, small_send, small_recv,
):
    tokens = q_in.shape[1]
    rows = clip_in.shape[0]
    scalars = [
        pltpu.make_async_copy(clip_ids_in, clip_ids, load.at[2]),
        pltpu.make_async_copy(text_ids_in, text_ids, load.at[3]),
    ]
    for copy in scalars:
        copy.start()
    full = tokens * SEQ
    s = lax.axis_index("seq")
    b = lax.axis_index("batch")
    z, y_hi = s // 2, s % 2
    y_lo, x, c = b // (NX * NC), (b // NC) % NX, b % NC
    y = y_hi * 2 + y_lo

    def seq_peer(k):
        return (lax.rem(s + k, SEQ), b)

    def x_peer(k):
        return (s, (y_lo * NX + lax.rem(x + k, NX)) * NC + c)

    def y_peer(k):
        other = lax.rem(y + k, NY)
        return (z * 2 + other // 2, ((other % 2) * NX + x) * NC + c)

    y_near = (s, b + (1 - 2 * y_lo) * NX * NC)
    y_far = (s + 1 - 2 * y_hi, b)
    c_peer = (s, b + 1 - 2 * c)

    def z_peer(k):
        return (lax.rem(z + k, NZ) * 2 + y_hi, b)

    barrier = pltpu.get_barrier_semaphore()

    def greet(peer):
        pl.semaphore_signal(barrier, inc=1, device_id=peer, device_id_type=MESH)

    for k in range(1, SEQ):
        greet(seq_peer(k))
    for k in range(1, NX):
        greet(x_peer(k))
    greet(c_peer)
    greet(y_peer(1))
    greet(y_peer(3))

    for copy in scalars:
        copy.wait()
    clip_y_ids[aligned(y, rows), :] = column_of_ids(clip_ids, rows)
    text_z_ids[aligned(z, rows), :] = column_of_ids(text_ids, rows)
    clip_own = aligned(y, rows)
    text_own = aligned(z, rows)
    clip_load = pltpu.make_async_copy(clip_in, clip_y.at[clip_own], load.at[0])
    text_load = pltpu.make_async_copy(text_in, text_z.at[text_own], load.at[1])
    clip_load.start()
    text_load.start()

    pl.semaphore_wait(barrier, SEQ - 1 + NX - 1 + 3)

    def send(src, dst, index, peer):
        pltpu.make_async_remote_copy(
            src_ref=src, dst_ref=dst, send_sem=small_send.at[index], recv_sem=small_recv.at[index],
            device_id=peer, device_id_type=MESH,
        ).start()

    for k in range(1, NY):
        send(clip_in, clip_y.at[clip_own], 0, y_peer(k))
        send(clip_y_ids.at[clip_own], clip_y_ids.at[clip_own], 1, y_peer(k))
    for k in range(1, NZ):
        send(text_in, text_z.at[text_own], 2, z_peer(k))
        send(text_z_ids.at[text_own], text_z_ids.at[text_own], 3, z_peer(k))

    ins = (k_in, q_in, v_in, d_in)

    def send_head(h):
        for a, ref in enumerate(ins):
            mine = aligned(s, tokens)
            pltpu.make_async_copy(
                ref.at[0, :, aligned(s * HEADS_HERE + h, HD)], land.at[h, a, mine], in_local.at[h, a]
            ).start()

            def to_peer(k, carry):
                peer = seq_peer(k)
                pltpu.make_async_remote_copy(
                    src_ref=ref.at[0, :, aligned(peer[0] * HEADS_HERE + h, HD)],
                    dst_ref=land.at[h, a, mine],
                    send_sem=in_send.at[h, a], recv_sem=in_recv.at[h, a],
                    device_id=peer, device_id_type=MESH,
                ).start()
                return carry

            lax.fori_loop(1, SEQ, to_peer, 0)

    others = full - tokens

    def wait_sent(h):
        for a in range(4):
            wait_for(land.at[h, a, pl.ds(0, others)], in_send.at[h, a])

    def wait_head(h, a):
        wait_for(land.at[h, a, pl.ds(0, others)], in_recv.at[h, a])
        wait_for(land.at[h, a, pl.ds(0, tokens)], in_local.at[h, a])

    wait_for(clip_y.at[pl.ds(0, 3 * rows)], small_recv.at[0])
    wait_for(clip_y_ids.at[pl.ds(0, 3 * rows)], small_recv.at[1])
    wait_for(text_z.at[pl.ds(0, 3 * rows)], small_recv.at[2])
    wait_for(text_z_ids.at[pl.ds(0, 3 * rows)], small_recv.at[3])

    send_head(0)

    group = NY * rows
    clip_load.wait()
    text_load.wait()
    for k in range(1, NX):
        send(clip_y, clip_x.at[aligned(x, group)], 4, x_peer(k))
        send(clip_y_ids, clip_x_ids.at[aligned(x, group)], 5, x_peer(k))
    clip_x[aligned(x, group), :] = clip_y[...]
    clip_x_ids[aligned(x, group), :] = clip_y_ids[...]
    send(text_z, text_c.at[aligned(c, group)], 6, c_peer)
    send(text_z_ids, text_c_ids.at[aligned(c, group)], 7, c_peer)
    text_c[aligned(c, group), :] = text_z[...]
    text_c_ids[aligned(c, group), :] = text_z_ids[...]

    wait_for(text_c.at[pl.ds(0, group)], small_recv.at[6])
    wait_for(text_c_ids.at[pl.ds(0, group)], small_recv.at[7])
    wait_for(clip_x.at[pl.ds(0, 3 * group)], small_recv.at[4])
    wait_for(clip_x_ids.at[pl.ds(0, 3 * group)], small_recv.at[5])
    scale = scale_ref[0]
    offset = bias_ref[0]
    clip_all = unit_rows(clip_x[...])[0].astype(BF16)
    text_all = unit_rows(text_c[...])[0].astype(BF16)
    logits = scale * nt(clip_all, text_all) + offset
    text_row = jnp.transpose(text_c_ids[...].astype(F32))[0:1, :]
    sign = jnp.where(clip_x_ids[...].astype(F32) == text_row, F32(1.0), F32(-1.0))
    turned = -sign * logits
    small = jnp.exp(-jnp.abs(turned))
    sigmoid = jnp.where(turned >= 0, F32(1.0), small) / (1.0 + small)
    loss_here = jnp.sum(jnp.maximum(turned, 0.0) + jnp.log1p(small))
    pair_grad = (scale * -sign * sigmoid).astype(BF16)
    text_part = tn(pair_grad, clip_all)
    for j in range(NC):
        dc_send[j, 0:group] = text_part[j * group : (j + 1) * group]
        dc_send[j, group : group + 8] = jnp.full((8, text_part.shape[1]), loss_here, F32)
    send(dc_send.at[1 - c], dc_recv, 8, c_peer)
    clip_part = nn(pair_grad, text_all)
    for j in range(NX):
        dx_send[j, 0:group] = clip_part[j * group : (j + 1) * group]
    wait_for(dc_recv, small_recv.at[8])
    text_sum = dc_send[c] + dc_recv[...]
    text_across = across(unit_rows(text_z[...])[0], text_sum[0:group])
    for j in range(NZ):
        dt_own[j] = text_across[j * rows : (j + 1) * rows]
        dt_send[j] = dt_own[j].astype(BF16)
    for j in range(NX):
        dx_send[j, group : group + 8] = text_sum[group : group + 8]
    for k in range(1, NX):
        send(dx_send.at[lax.rem(x + k, NX)], dx_recv.at[x], 9, x_peer(k))
    for k in range(1, NZ):
        send(dt_send.at[lax.rem(z + k, NZ)], dt_recv.at[z], 10, z_peer(k))
    dx_recv[x] = dx_send[x]
    dt_recv[z] = jnp.zeros(dt_recv.shape[1:], BF16)

    wait_sent(0)
    send_head(1)

    def attend(h):
        k_all, q_all, v_all, d_all = (land.at[h, a] for a in range(4))
        for a in range(4):
            wait_head(h, a)
        dk_sum[...] = jnp.zeros_like(dk_sum)
        dv_sum[...] = jnp.zeros_like(dv_sum)

        def step(i, carry):
            r = aligned(i, BLOCK_Q)
            q = q_all[r, :]
            d = d_all[r, :]
            raw_scores = nt(q, k_all[...])
            top = jnp.max(raw_scores, axis=1, keepdims=True)
            expo = jnp.exp2(raw_scores * EXP2_SCALE - top * EXP2_SCALE)
            total = jnp.sum(expo, axis=1, keepdims=True)
            probs = expo * (1.0 / total)
            probs_b = probs.astype(BF16)
            out = nn(probs_b, v_all[...]).astype(BF16)
            res[h, 0, r, :] = out
            dv_sum[...] += tn(probs_b, d)
            dprobs = nt(d, v_all[...])
            delta = jnp.sum(d.astype(F32) * out.astype(F32), axis=1, keepdims=True)
            dscores = (probs * (dprobs - delta)).astype(BF16)
            res[h, 1, r, :] = (nn(dscores, k_all[...]) * INV_ROOT).astype(BF16)
            dk_sum[...] += tn(dscores, q)
            return carry

        lax.fori_loop(0, full // BLOCK_Q, step, 0)
        res[h, 2] = (dk_sum[...] * INV_ROOT).astype(BF16)
        res[h, 3] = dv_sum[...].astype(BF16)

    outs = (o_out, dq_out, dk_out, dv_out)

    def return_head(h):
        for a, ref in enumerate(outs):
            columns = aligned(s * HEADS_HERE + h, HD)
            pltpu.make_async_copy(
                res.at[h, a, aligned(s, tokens)], ref.at[0, :, columns], out_local.at[a]
            ).start()

            def to_peer(k, carry):
                peer = seq_peer(k)
                pltpu.make_async_remote_copy(
                    src_ref=res.at[h, a, aligned(peer[0], tokens)],
                    dst_ref=ref.at[0, :, columns],
                    send_sem=out_send.at[a], recv_sem=out_recv.at[a],
                    device_id=peer, device_id_type=MESH,
                ).start()
                return carry

            lax.fori_loop(1, SEQ, to_peer, 0)

    attend(0)
    return_head(0)

    wait_for(dx_recv.at[pl.ds(0, NX - 1)], small_recv.at[9])
    clip_sum = dx_recv[0]
    for j in range(1, NX):
        clip_sum = clip_sum + dx_recv[j]
    clip_across = across(unit_rows(clip_y[...])[0], clip_sum[0:group])
    for j in range(2):
        near_own[j, 0:rows] = clip_across[j * rows : (j + 1) * rows]
        near_own[j, rows : 2 * rows] = clip_across[(2 + j) * rows : (3 + j) * rows]
        near_send[j] = near_own[j].astype(BF16)
    loss_y[0] = clip_sum[group : group + 8, 0:HD]
    send(near_send.at[1 - y_lo], near_recv, 11, y_near)
    send(loss_y.at[0], loss_y.at[1], 13, y_near)

    attend(1)

    wait_for(near_recv, small_recv.at[11])
    wait_for(loss_y.at[0], small_recv.at[13])
    clip_sum = near_own[y_lo] + near_recv[...].astype(F32)
    for j in range(2):
        far_own[j] = clip_sum[j * rows : (j + 1) * rows]
        far_send[j] = far_own[j].astype(BF16)
    loss_recv[s] = loss_y[0] + loss_y[1]
    send(far_send.at[1 - y_hi], far_recv, 14, y_far)
    for k in range(1, SEQ):
        send(loss_recv.at[s], loss_recv.at[s], 12, seq_peer(k))

    return_head(1)

    wait_for(far_recv, small_recv.at[14])
    clip_sum = far_own[y_hi] + far_recv[...].astype(F32)
    grad_clip[...] = raw_grad(clip_y[clip_own, :], clip_sum)

    wait_for(dt_recv.at[pl.ds(0, NZ - 1)], small_recv.at[10])
    text_sum = dt_own[z]
    for j in range(NZ):
        text_sum = text_sum + dt_recv[j].astype(F32)
    grad_text[...] = raw_grad(text_z[text_own, :], text_sum)

    wait_for(loss_recv.at[pl.ds(0, SEQ - 1)], small_recv.at[12])
    loss_sum = loss_recv[0]
    for j in range(1, SEQ):
        loss_sum = loss_sum + loss_recv[j]
    loss_out[...] = loss_sum / (rows * SEQ * BATCH)

    for index, ref in (
        (0, clip_y.at[pl.ds(0, 3 * rows)]),
        (1, clip_y_ids.at[pl.ds(0, 3 * rows)]),
        (2, text_z.at[pl.ds(0, 3 * rows)]),
        (3, text_z_ids.at[pl.ds(0, 3 * rows)]),
        (4, clip_x.at[pl.ds(0, 3 * group)]),
        (5, clip_x_ids.at[pl.ds(0, 3 * group)]),
        (6, text_c.at[pl.ds(0, group)]),
        (7, text_c_ids.at[pl.ds(0, group)]),
        (8, dc_recv),
        (9, dx_recv.at[pl.ds(0, NX - 1)]),
        (10, dt_recv.at[pl.ds(0, NZ - 1)]),
        (11, near_recv),
        (13, loss_y.at[0]),
        (14, far_recv),
        (12, loss_recv.at[pl.ds(0, SEQ - 1)]),
    ):
        wait_for(ref, small_send.at[index])
    wait_sent(1)
    remote = HEADS_HERE * (SEQ - 1) * HD
    for a, ref in enumerate(outs):
        wait_for(ref.at[0, :, pl.ds(0, HEADS_HERE * HD)], out_local.at[a])
        wait_for(ref.at[0, :, pl.ds(0, remote)], out_send.at[a])
        wait_for(ref.at[0, :, pl.ds(0, remote)], out_recv.at[a])


def hand_over(*refs):
    sources, targets, loss, sems = refs[:7], refs[7:14], refs[14], refs[15]
    copies = [pltpu.make_async_copy(sources[a], targets[a], sems.at[a]) for a in range(6)]
    for copy in copies:
        copy.start()
    loss[0] = sources[6][0, 0]
    copies.append(pltpu.make_async_copy(loss, targets[6], sems.at[6]))
    copies[-1].start()
    for copy in copies:
        copy.wait()


def body(queries, key_vectors, value_vectors, cotangent, clip_raw, text_raw, clip_video, text_video, logit_scale, logit_bias):
    tokens = queries.shape[1]
    full = tokens * SEQ
    rows, width = clip_raw.shape
    in_hbm = pl.BlockSpec(memory_space=pl.ANY)
    in_vmem = pl.BlockSpec(memory_space=pltpu.VMEM)
    in_smem = pl.BlockSpec(memory_space=pltpu.SMEM)
    group = NY * rows
    dma = pltpu.SemaphoreType.DMA
    in_place = (queries, key_vectors, value_vectors, cotangent, clip_raw, text_raw, clip_video, text_video)
    results = pl.pallas_call(
        kernel,
        out_shape=(
            *[pltpu.VMEM(queries.shape, BF16)] * 4,
            pltpu.VMEM((rows, width), F32),
            pltpu.VMEM((rows, width), F32),
            pltpu.VMEM((8, HD), F32),
        ),
        in_specs=[in_hbm] * 8 + [in_smem] * 2,
        out_specs=[in_vmem] * 7,
        scratch_shapes=[
            pltpu.SMEM((rows,), jnp.int32),
            pltpu.SMEM((rows,), jnp.int32),
            dma((4,)),
            pltpu.VMEM((HEADS_HERE, 4, full, HD), BF16),
            pltpu.VMEM((HEADS_HERE, 4, full, HD), BF16),
            pltpu.VMEM((full, HD), F32),
            pltpu.VMEM((full, HD), F32),
            pltpu.VMEM((group, width), BF16),
            pltpu.VMEM((group, HD), jnp.int32),
            pltpu.VMEM((NX * group, width), BF16),
            pltpu.VMEM((NX * group, HD), jnp.int32),
            pltpu.VMEM((NZ * rows, width), BF16),
            pltpu.VMEM((NZ * rows, HD), jnp.int32),
            pltpu.VMEM((NC * NZ * rows, width), BF16),
            pltpu.VMEM((NC * NZ * rows, HD), jnp.int32),
            pltpu.VMEM((NC, group + 8, width), F32),
            pltpu.VMEM((group + 8, width), F32),
            pltpu.VMEM((NX, group + 8, width), F32),
            pltpu.VMEM((NX, group + 8, width), F32),
            pltpu.VMEM((2, 2 * rows, width), F32),
            pltpu.VMEM((2, 2 * rows, width), BF16),
            pltpu.VMEM((2 * rows, width), BF16),
            pltpu.VMEM((2, rows, width), F32),
            pltpu.VMEM((2, rows, width), BF16),
            pltpu.VMEM((rows, width), BF16),
            pltpu.VMEM((2, 8, HD), F32),
            pltpu.VMEM((NZ, rows, width), F32),
            pltpu.VMEM((NZ, rows, width), BF16),
            pltpu.VMEM((NZ, rows, width), BF16),
            pltpu.VMEM((SEQ, 8, HD), F32),
            dma((HEADS_HERE, 4)),
            dma((HEADS_HERE, 4)),
            dma((HEADS_HERE, 4)),
            dma((4,)),
            dma((4,)),
            dma((4,)),
            dma((15,)),
            dma((15,)),
        ],
        compiler_params=pltpu.CompilerParams(
            collective_id=0, has_side_effects=True, vmem_limit_bytes=48 * 2**20
        ),
        cost_estimate=pl.CostEstimate(
            flops=HEADS_HERE * 12 * full * full * HD, bytes_accessed=8 * full * HD * 2, transcendentals=HEADS_HERE * full * full
        ),
        name="tower",
    )(*[pltpu.with_memory_space_constraint(array, pltpu.HBM) for array in in_place], logit_scale, logit_bias)
    return pl.pallas_call(
        hand_over,
        out_shape=(
            *[jax.ShapeDtypeStruct(queries.shape, BF16)] * 4,
            jax.ShapeDtypeStruct((rows, width), F32),
            jax.ShapeDtypeStruct((rows, width), F32),
            jax.ShapeDtypeStruct((1,), F32),
        ),
        in_specs=[in_vmem] * 7,
        out_specs=[in_hbm] * 7,
        scratch_shapes=[pltpu.SMEM((1,), F32), dma((7,))],
        name="hand_over",
    )(*[pltpu.with_memory_space_constraint(array, pltpu.VMEM) for array in results])


def solution(mesh):
    tokens = P("batch", "seq", None)
    embeddings = P(("seq", "batch"), None)
    ids = P(("seq", "batch"))
    return jax.shard_map(
        body,
        mesh=mesh,
        in_specs=(tokens,) * 4 + (embeddings,) * 2 + (ids,) * 2 + (P(), P()),
        out_specs=(tokens,) * 4 + (embeddings,) * 2 + (P(),),
        check_vma=False,
    )
```

```python
import functools
import math

import jax
import jax.numpy as jnp
from jax import lax
from jax.experimental import pallas as pl
from jax.experimental.pallas import tpu as pltpu
from jax.sharding import PartitionSpec as P

MESH = pl.DeviceIdType.MESH
F32 = jnp.float32
BF16 = jnp.bfloat16

HD = 128
SEQ = 8
BATCH = 16
NZ = 4
NY = 4
NX = 4
NC = 2
HEADS_HERE = 2
BLOCK_Q = 512

INV_ROOT = 1.0 / math.sqrt(HD)
EXP2_SCALE = INV_ROOT * math.log2(math.e)


def nt(a, b):
    return lax.dot_general(a, b, (((1,), (1,)), ((), ())), preferred_element_type=F32)


def nn(a, b):
    return lax.dot_general(a, b, (((1,), (0,)), ((), ())), preferred_element_type=F32)


def tn(a, b):
    return lax.dot_general(a, b, (((0,), (0,)), ((), ())), preferred_element_type=F32)


def aligned(index, size):
    return pl.ds(pl.multiple_of(index * size, size), size)


def unit_rows(raw):
    rawf = raw.astype(F32)
    norm = jnp.sqrt(jnp.sum(rawf * rawf, axis=1, keepdims=True) + 1e-06)
    return (rawf / norm, norm)


def across(unit, direction):
    return direction - unit * jnp.sum(unit * direction, axis=1, keepdims=True)


def raw_grad(raw, direction):
    unit, norm = unit_rows(raw)
    return across(unit, direction) / norm


def wait_for(ref, sem):
    pltpu.make_async_copy(ref, ref, sem).wait()


def column_of_ids(ids_ref, rows):
    row = lax.broadcasted_iota(jnp.int32, (rows, HD), 0)
    column = jnp.zeros((rows, HD), jnp.int32)
    for i in range(rows):
        column = jnp.where(row == i, ids_ref[i], column)
    return column


def kernel(
    q_in, k_in, v_in, d_in, clip_in, text_in, clip_ids_in, text_ids_in, scale_ref, bias_ref,
    o_out, dq_out, dk_out, dv_out, grad_clip, grad_text, loss_out,
    clip_ids, text_ids, load, land, res, dk_sum, dv_sum,
    clip_y, clip_y_ids, clip_x, clip_x_ids, text_z, text_z_ids, text_c, text_c_ids,
    dc_send, dc_recv, dx_send, dx_recv, near_own, near_send, near_recv, far_own, far_send, far_recv, loss_y, dt_own, dt_send, dt_recv, loss_recv,
    in_send, in_recv, in_local, out_send, out_recv, out_local, small_send, small_recv,
):
    tokens = q_in.shape[1]
    rows = clip_in.shape[0]
    scalars = [
        pltpu.make_async_copy(clip_ids_in, clip_ids, load.at[2]),
        pltpu.make_async_copy(text_ids_in, text_ids, load.at[3]),
    ]
    for copy in scalars:
        copy.start()
    full = tokens * SEQ
    s = lax.axis_index("seq")
    b = lax.axis_index("batch")
    z, y_hi = s // 2, s % 2
    y_lo, x, c = b // (NX * NC), (b // NC) % NX, b % NC
    y = y_hi * 2 + y_lo

    def seq_peer(k):
        return (lax.rem(s + k, SEQ), b)

    def x_peer(k):
        return (s, (y_lo * NX + lax.rem(x + k, NX)) * NC + c)

    def y_peer(k):
        other = lax.rem(y + k, NY)
        return (z * 2 + other // 2, ((other % 2) * NX + x) * NC + c)

    y_near = (s, b + (1 - 2 * y_lo) * NX * NC)
    y_far = (s + 1 - 2 * y_hi, b)
    c_peer = (s, b + 1 - 2 * c)

    def z_peer(k):
        return (lax.rem(z + k, NZ) * 2 + y_hi, b)

    barrier = pltpu.get_barrier_semaphore()

    def greet(peer):
        pl.semaphore_signal(barrier, inc=1, device_id=peer, device_id_type=MESH)

    for k in range(1, SEQ):
        greet(seq_peer(k))
    for k in range(1, NX):
        greet(x_peer(k))
    greet(c_peer)
    greet(y_peer(1))
    greet(y_peer(3))

    for copy in scalars:
        copy.wait()
    clip_y_ids[aligned(y, rows), :] = column_of_ids(clip_ids, rows)
    text_z_ids[aligned(z, rows), :] = column_of_ids(text_ids, rows)
    clip_own = aligned(y, rows)
    text_own = aligned(z, rows)
    clip_load = pltpu.make_async_copy(clip_in, clip_y.at[clip_own], load.at[0])
    text_load = pltpu.make_async_copy(text_in, text_z.at[text_own], load.at[1])
    clip_load.start()
    text_load.start()

    pl.semaphore_wait(barrier, SEQ - 1 + NX - 1 + 3)

    def send(src, dst, index, peer):
        pltpu.make_async_remote_copy(
            src_ref=src, dst_ref=dst, send_sem=small_send.at[index], recv_sem=small_recv.at[index],
            device_id=peer, device_id_type=MESH,
        ).start()

    for k in range(1, NY):
        send(clip_in, clip_y.at[clip_own], 0, y_peer(k))
        send(clip_y_ids.at[clip_own], clip_y_ids.at[clip_own], 1, y_peer(k))
    for k in range(1, NZ):
        send(text_in, text_z.at[text_own], 2, z_peer(k))
        send(text_z_ids.at[text_own], text_z_ids.at[text_own], 3, z_peer(k))

    ins = (k_in, q_in, v_in, d_in)

    def send_head(h):
        for a, ref in enumerate(ins):
            mine = aligned(s, tokens)
            pltpu.make_async_copy(
                ref.at[0, :, aligned(s * HEADS_HERE + h, HD)], land.at[h, a, mine], in_local.at[h, a]
            ).start()

            def to_peer(k, carry):
                peer = seq_peer(k)
                pltpu.make_async_remote_copy(
                    src_ref=ref.at[0, :, aligned(peer[0] * HEADS_HERE + h, HD)],
                    dst_ref=land.at[h, a, mine],
                    send_sem=in_send.at[h, a], recv_sem=in_recv.at[h, a],
                    device_id=peer, device_id_type=MESH,
                ).start()
                return carry

            lax.fori_loop(1, SEQ, to_peer, 0)

    others = full - tokens

    def wait_sent(h):
        for a in range(4):
            wait_for(land.at[h, a, pl.ds(0, others)], in_send.at[h, a])

    def wait_head(h, a):
        wait_for(land.at[h, a, pl.ds(0, others)], in_recv.at[h, a])
        wait_for(land.at[h, a, pl.ds(0, tokens)], in_local.at[h, a])

    wait_for(clip_y.at[pl.ds(0, 3 * rows)], small_recv.at[0])
    wait_for(clip_y_ids.at[pl.ds(0, 3 * rows)], small_recv.at[1])

    send_head(0)

    group = NY * rows
    clip_load.wait()
    text_load.wait()
    for k in range(1, NX):
        send(clip_y, clip_x.at[aligned(x, group)], 4, x_peer(k))
        send(clip_y_ids, clip_x_ids.at[aligned(x, group)], 5, x_peer(k))
    clip_x[aligned(x, group), :] = clip_y[...]
    clip_x_ids[aligned(x, group), :] = clip_y_ids[...]
    wait_for(text_z.at[pl.ds(0, 3 * rows)], small_recv.at[2])
    wait_for(text_z_ids.at[pl.ds(0, 3 * rows)], small_recv.at[3])
    send(text_z, text_c.at[aligned(c, group)], 6, c_peer)
    send(text_z_ids, text_c_ids.at[aligned(c, group)], 7, c_peer)
    text_c[aligned(c, group), :] = text_z[...]
    text_c_ids[aligned(c, group), :] = text_z_ids[...]

    wait_for(text_c.at[pl.ds(0, group)], small_recv.at[6])
    wait_for(text_c_ids.at[pl.ds(0, group)], small_recv.at[7])
    wait_for(clip_x.at[pl.ds(0, 3 * group)], small_recv.at[4])
    wait_for(clip_x_ids.at[pl.ds(0, 3 * group)], small_recv.at[5])
    scale = scale_ref[0]
    offset = bias_ref[0]
    clip_all = unit_rows(clip_x[...])[0].astype(BF16)
    text_all = unit_rows(text_c[...])[0].astype(BF16)
    logits = scale * nt(clip_all, text_all) + offset
    text_row = jnp.transpose(text_c_ids[...].astype(F32))[0:1, :]
    sign = jnp.where(clip_x_ids[...].astype(F32) == text_row, F32(1.0), F32(-1.0))
    turned = -sign * logits
    small = jnp.exp(-jnp.abs(turned))
    sigmoid = jnp.where(turned >= 0, F32(1.0), small) / (1.0 + small)
    loss_here = jnp.sum(jnp.maximum(turned, 0.0) + jnp.log1p(small))
    pair_grad = (scale * -sign * sigmoid).astype(BF16)
    text_part = tn(pair_grad, clip_all)
    for j in range(NC):
        dc_send[j, 0:group] = text_part[j * group : (j + 1) * group]
        dc_send[j, group : group + 8] = jnp.full((8, text_part.shape[1]), loss_here, F32)
    send(dc_send.at[1 - c], dc_recv, 8, c_peer)
    clip_part = nn(pair_grad, text_all)
    for j in range(NX):
        dx_send[j, 0:group] = clip_part[j * group : (j + 1) * group]
    wait_for(dc_recv, small_recv.at[8])
    text_sum = dc_send[c] + dc_recv[...]
    text_across = across(unit_rows(text_z[...])[0], text_sum[0:group])
    for j in range(NZ):
        dt_own[j] = text_across[j * rows : (j + 1) * rows]
        dt_send[j] = dt_own[j].astype(BF16)
    for j in range(NX):
        dx_send[j, group : group + 8] = text_sum[group : group + 8]
    for k in range(1, NX):
        send(dx_send.at[lax.rem(x + k, NX)], dx_recv.at[x], 9, x_peer(k))
    for k in range(1, NZ):
        send(dt_send.at[lax.rem(z + k, NZ)], dt_recv.at[z], 10, z_peer(k))
    dx_recv[x] = dx_send[x]
    dt_recv[z] = jnp.zeros(dt_recv.shape[1:], BF16)

    wait_sent(0)
    send_head(1)

    def attend(h):
        k_all, q_all, v_all, d_all = (land.at[h, a] for a in range(4))
        for a in range(4):
            wait_head(h, a)
        dk_sum[...] = jnp.zeros_like(dk_sum)
        dv_sum[...] = jnp.zeros_like(dv_sum)

        def step(i, carry):
            r = aligned(i, BLOCK_Q)
            q = q_all[r, :]
            d = d_all[r, :]
            raw_scores = nt(q, k_all[...])
            top = jnp.max(raw_scores, axis=1, keepdims=True)
            expo = jnp.exp2(raw_scores * EXP2_SCALE - top * EXP2_SCALE)
            total = jnp.sum(expo, axis=1, keepdims=True)
            probs = expo * (1.0 / total)
            probs_b = probs.astype(BF16)
            out = nn(probs_b, v_all[...]).astype(BF16)
            res[h, 0, r, :] = out
            dv_sum[...] += tn(probs_b, d)
            dprobs = nt(d, v_all[...])
            delta = jnp.sum(d.astype(F32) * out.astype(F32), axis=1, keepdims=True)
            dscores = (probs * (dprobs - delta)).astype(BF16)
            res[h, 1, r, :] = (nn(dscores, k_all[...]) * INV_ROOT).astype(BF16)
            dk_sum[...] += tn(dscores, q)
            return carry

        lax.fori_loop(0, full // BLOCK_Q, step, 0)
        res[h, 2] = (dk_sum[...] * INV_ROOT).astype(BF16)
        res[h, 3] = dv_sum[...].astype(BF16)

    outs = (o_out, dq_out, dk_out, dv_out)

    def return_head(h):
        for a, ref in enumerate(outs):
            columns = aligned(s * HEADS_HERE + h, HD)
            pltpu.make_async_copy(
                res.at[h, a, aligned(s, tokens)], ref.at[0, :, columns], out_local.at[a]
            ).start()

            def to_peer(k, carry):
                peer = seq_peer(k)
                pltpu.make_async_remote_copy(
                    src_ref=res.at[h, a, aligned(peer[0], tokens)],
                    dst_ref=ref.at[0, :, columns],
                    send_sem=out_send.at[a], recv_sem=out_recv.at[a],
                    device_id=peer, device_id_type=MESH,
                ).start()
                return carry

            lax.fori_loop(1, SEQ, to_peer, 0)

    attend(0)
    return_head(0)

    wait_for(dx_recv.at[pl.ds(0, NX - 1)], small_recv.at[9])
    clip_sum = dx_recv[0]
    for j in range(1, NX):
        clip_sum = clip_sum + dx_recv[j]
    clip_across = across(unit_rows(clip_y[...])[0], clip_sum[0:group])
    for j in range(2):
        near_own[j, 0:rows] = clip_across[j * rows : (j + 1) * rows]
        near_own[j, rows : 2 * rows] = clip_across[(2 + j) * rows : (3 + j) * rows]
        near_send[j] = near_own[j].astype(BF16)
    loss_y[0] = clip_sum[group : group + 8, 0:HD]
    send(near_send.at[1 - y_lo], near_recv, 11, y_near)
    send(loss_y.at[0], loss_y.at[1], 13, y_near)

    attend(1)

    wait_for(near_recv, small_recv.at[11])
    wait_for(loss_y.at[0], small_recv.at[13])
    clip_sum = near_own[y_lo] + near_recv[...].astype(F32)
    for j in range(2):
        far_own[j] = clip_sum[j * rows : (j + 1) * rows]
        far_send[j] = far_own[j].astype(BF16)
    loss_recv[s] = loss_y[0] + loss_y[1]
    send(far_send.at[1 - y_hi], far_recv, 14, y_far)
    for k in range(1, SEQ):
        send(loss_recv.at[s], loss_recv.at[s], 12, seq_peer(k))

    return_head(1)

    wait_for(far_recv, small_recv.at[14])
    clip_sum = far_own[y_hi] + far_recv[...].astype(F32)
    grad_clip[...] = raw_grad(clip_y[clip_own, :], clip_sum)

    wait_for(dt_recv.at[pl.ds(0, NZ - 1)], small_recv.at[10])
    text_sum = dt_own[z]
    for j in range(NZ):
        text_sum = text_sum + dt_recv[j].astype(F32)
    grad_text[...] = raw_grad(text_z[text_own, :], text_sum)

    wait_for(loss_recv.at[pl.ds(0, SEQ - 1)], small_recv.at[12])
    loss_sum = loss_recv[0]
    for j in range(1, SEQ):
        loss_sum = loss_sum + loss_recv[j]
    loss_out[...] = loss_sum / (rows * SEQ * BATCH)

    for index, ref in (
        (0, clip_y.at[pl.ds(0, 3 * rows)]),
        (1, clip_y_ids.at[pl.ds(0, 3 * rows)]),
        (2, text_z.at[pl.ds(0, 3 * rows)]),
        (3, text_z_ids.at[pl.ds(0, 3 * rows)]),
        (4, clip_x.at[pl.ds(0, 3 * group)]),
        (5, clip_x_ids.at[pl.ds(0, 3 * group)]),
        (6, text_c.at[pl.ds(0, group)]),
        (7, text_c_ids.at[pl.ds(0, group)]),
        (8, dc_recv),
        (9, dx_recv.at[pl.ds(0, NX - 1)]),
        (10, dt_recv.at[pl.ds(0, NZ - 1)]),
        (11, near_recv),
        (13, loss_y.at[0]),
        (14, far_recv),
        (12, loss_recv.at[pl.ds(0, SEQ - 1)]),
    ):
        wait_for(ref, small_send.at[index])
    wait_sent(1)
    remote = HEADS_HERE * (SEQ - 1) * HD
    for a, ref in enumerate(outs):
        wait_for(ref.at[0, :, pl.ds(0, HEADS_HERE * HD)], out_local.at[a])
        wait_for(ref.at[0, :, pl.ds(0, remote)], out_send.at[a])
        wait_for(ref.at[0, :, pl.ds(0, remote)], out_recv.at[a])


def hand_over(*refs):
    sources, targets, loss, sems = refs[:7], refs[7:14], refs[14], refs[15]
    copies = [pltpu.make_async_copy(sources[a], targets[a], sems.at[a]) for a in range(6)]
    for copy in copies:
        copy.start()
    loss[0] = sources[6][0, 0]
    copies.append(pltpu.make_async_copy(loss, targets[6], sems.at[6]))
    copies[-1].start()
    for copy in copies:
        copy.wait()


def body(queries, key_vectors, value_vectors, cotangent, clip_raw, text_raw, clip_video, text_video, logit_scale, logit_bias):
    tokens = queries.shape[1]
    full = tokens * SEQ
    rows, width = clip_raw.shape
    in_hbm = pl.BlockSpec(memory_space=pl.ANY)
    in_vmem = pl.BlockSpec(memory_space=pltpu.VMEM)
    in_smem = pl.BlockSpec(memory_space=pltpu.SMEM)
    group = NY * rows
    dma = pltpu.SemaphoreType.DMA
    in_place = (queries, key_vectors, value_vectors, cotangent, clip_raw, text_raw, clip_video, text_video)
    results = pl.pallas_call(
        kernel,
        out_shape=(
            *[pltpu.VMEM(queries.shape, BF16)] * 4,
            pltpu.VMEM((rows, width), F32),
            pltpu.VMEM((rows, width), F32),
            pltpu.VMEM((8, HD), F32),
        ),
        in_specs=[in_hbm] * 8 + [in_smem] * 2,
        out_specs=[in_vmem] * 7,
        scratch_shapes=[
            pltpu.SMEM((rows,), jnp.int32),
            pltpu.SMEM((rows,), jnp.int32),
            dma((4,)),
            pltpu.VMEM((HEADS_HERE, 4, full, HD), BF16),
            pltpu.VMEM((HEADS_HERE, 4, full, HD), BF16),
            pltpu.VMEM((full, HD), F32),
            pltpu.VMEM((full, HD), F32),
            pltpu.VMEM((group, width), BF16),
            pltpu.VMEM((group, HD), jnp.int32),
            pltpu.VMEM((NX * group, width), BF16),
            pltpu.VMEM((NX * group, HD), jnp.int32),
            pltpu.VMEM((NZ * rows, width), BF16),
            pltpu.VMEM((NZ * rows, HD), jnp.int32),
            pltpu.VMEM((NC * NZ * rows, width), BF16),
            pltpu.VMEM((NC * NZ * rows, HD), jnp.int32),
            pltpu.VMEM((NC, group + 8, width), F32),
            pltpu.VMEM((group + 8, width), F32),
            pltpu.VMEM((NX, group + 8, width), F32),
            pltpu.VMEM((NX, group + 8, width), F32),
            pltpu.VMEM((2, 2 * rows, width), F32),
            pltpu.VMEM((2, 2 * rows, width), BF16),
            pltpu.VMEM((2 * rows, width), BF16),
            pltpu.VMEM((2, rows, width), F32),
            pltpu.VMEM((2, rows, width), BF16),
            pltpu.VMEM((rows, width), BF16),
            pltpu.VMEM((2, 8, HD), F32),
            pltpu.VMEM((NZ, rows, width), F32),
            pltpu.VMEM((NZ, rows, width), BF16),
            pltpu.VMEM((NZ, rows, width), BF16),
            pltpu.VMEM((SEQ, 8, HD), F32),
            dma((HEADS_HERE, 4)),
            dma((HEADS_HERE, 4)),
            dma((HEADS_HERE, 4)),
            dma((4,)),
            dma((4,)),
            dma((4,)),
            dma((15,)),
            dma((15,)),
        ],
        compiler_params=pltpu.CompilerParams(
            collective_id=0, has_side_effects=True, vmem_limit_bytes=48 * 2**20
        ),
        cost_estimate=pl.CostEstimate(
            flops=HEADS_HERE * 12 * full * full * HD, bytes_accessed=8 * full * HD * 2, transcendentals=HEADS_HERE * full * full
        ),
        name="tower",
    )(*[pltpu.with_memory_space_constraint(array, pltpu.HBM) for array in in_place], logit_scale, logit_bias)
    return pl.pallas_call(
        hand_over,
        out_shape=(
            *[jax.ShapeDtypeStruct(queries.shape, BF16)] * 4,
            jax.ShapeDtypeStruct((rows, width), F32),
            jax.ShapeDtypeStruct((rows, width), F32),
            jax.ShapeDtypeStruct((1,), F32),
        ),
        in_specs=[in_vmem] * 7,
        out_specs=[in_hbm] * 7,
        scratch_shapes=[pltpu.SMEM((1,), F32), dma((7,))],
        name="hand_over",
    )(*[pltpu.with_memory_space_constraint(array, pltpu.VMEM) for array in results])


def solution(mesh):
    tokens = P("batch", "seq", None)
    embeddings = P(("seq", "batch"), None)
    ids = P(("seq", "batch"))
    return jax.shard_map(
        body,
        mesh=mesh,
        in_specs=(tokens,) * 4 + (embeddings,) * 2 + (ids,) * 2 + (P(), P()),
        out_specs=(tokens,) * 4 + (embeddings,) * 2 + (P(),),
        check_vma=False,
    )
```

```python
import functools
import math

import jax
import jax.numpy as jnp
from jax import lax
from jax.experimental import pallas as pl
from jax.experimental.pallas import tpu as pltpu
from jax.sharding import PartitionSpec as P

MESH = pl.DeviceIdType.MESH
F32 = jnp.float32
BF16 = jnp.bfloat16

HD = 128
SEQ = 8
BATCH = 16
NZ = 4
NY = 4
NX = 4
NC = 2
HEADS_HERE = 2
BLOCK_Q = 512

INV_ROOT = 1.0 / math.sqrt(HD)
EXP2_SCALE = INV_ROOT * math.log2(math.e)


def nt(a, b):
    return lax.dot_general(a, b, (((1,), (1,)), ((), ())), preferred_element_type=F32)


def nn(a, b):
    return lax.dot_general(a, b, (((1,), (0,)), ((), ())), preferred_element_type=F32)


def tn(a, b):
    return lax.dot_general(a, b, (((0,), (0,)), ((), ())), preferred_element_type=F32)


def aligned(index, size):
    return pl.ds(pl.multiple_of(index * size, size), size)


def unit_rows(raw):
    rawf = raw.astype(F32)
    norm = jnp.sqrt(jnp.sum(rawf * rawf, axis=1, keepdims=True) + 1e-06)
    return (rawf / norm, norm)


def across(unit, direction):
    return direction - unit * jnp.sum(unit * direction, axis=1, keepdims=True)


def raw_grad(raw, direction):
    unit, norm = unit_rows(raw)
    return across(unit, direction) / norm


def wait_for(ref, sem):
    pltpu.make_async_copy(ref, ref, sem).wait()


def column_of_ids(ids_ref, rows):
    row = lax.broadcasted_iota(jnp.int32, (rows, HD), 0)
    column = jnp.zeros((rows, HD), jnp.int32)
    for i in range(rows):
        column = jnp.where(row == i, ids_ref[i], column)
    return column


def kernel(
    q_in, k_in, v_in, d_in, clip_in, text_in, clip_ids_in, text_ids_in, scale_ref, bias_ref,
    o_out, dq_out, dk_out, dv_out, grad_clip, grad_text, loss_out,
    clip_ids, text_ids, load, land, res, dk_sum, dv_sum,
    clip_y, clip_y_ids, clip_x, clip_x_ids, text_z, text_z_ids, text_c, text_c_ids,
    dc_send, dc_recv, dx_send, dx_recv, near_own, near_send, near_recv, far_own, far_send, far_recv, loss_y, dt_own, dt_send, dt_recv, loss_recv,
    in_send, in_recv, in_local, out_send, out_recv, out_local, small_send, small_recv,
):
    tokens = q_in.shape[1]
    rows = clip_in.shape[0]
    scalars = [
        pltpu.make_async_copy(clip_ids_in, clip_ids, load.at[2]),
        pltpu.make_async_copy(text_ids_in, text_ids, load.at[3]),
    ]
    for copy in scalars:
        copy.start()
    full = tokens * SEQ
    s = lax.axis_index("seq")
    b = lax.axis_index("batch")
    z, y_hi = s // 2, s % 2
    y_lo, x, c = b // (NX * NC), (b // NC) % NX, b % NC
    y = y_hi * 2 + y_lo

    def seq_peer(k):
        return (lax.rem(s + k, SEQ), b)

    def x_peer(k):
        return (s, (y_lo * NX + lax.rem(x + k, NX)) * NC + c)

    def y_peer(k):
        other = lax.rem(y + k, NY)
        return (z * 2 + other // 2, ((other % 2) * NX + x) * NC + c)

    y_near = (s, b + (1 - 2 * y_lo) * NX * NC)
    y_far = (s + 1 - 2 * y_hi, b)
    c_peer = (s, b + 1 - 2 * c)

    def z_peer(k):
        return (lax.rem(z + k, NZ) * 2 + y_hi, b)

    barrier = pltpu.get_barrier_semaphore()

    def greet(peer):
        pl.semaphore_signal(barrier, inc=1, device_id=peer, device_id_type=MESH)

    for k in range(1, SEQ):
        greet(seq_peer(k))
    for k in range(1, NX):
        greet(x_peer(k))
    greet(c_peer)
    greet(y_peer(1))
    greet(y_peer(3))

    for copy in scalars:
        copy.wait()
    clip_y_ids[aligned(y, rows), :] = column_of_ids(clip_ids, rows)
    text_z_ids[aligned(z, rows), :] = column_of_ids(text_ids, rows)
    clip_own = aligned(y, rows)
    text_own = aligned(z, rows)
    clip_load = pltpu.make_async_copy(clip_in, clip_y.at[clip_own], load.at[0])
    text_load = pltpu.make_async_copy(text_in, text_z.at[text_own], load.at[1])
    clip_load.start()
    text_load.start()

    pl.semaphore_wait(barrier, SEQ - 1 + NX - 1 + 3)

    def send(src, dst, index, peer):
        pltpu.make_async_remote_copy(
            src_ref=src, dst_ref=dst, send_sem=small_send.at[index], recv_sem=small_recv.at[index],
            device_id=peer, device_id_type=MESH,
        ).start()

    for k in range(1, NY):
        send(clip_in, clip_y.at[clip_own], 0, y_peer(k))
        send(clip_y_ids.at[clip_own], clip_y_ids.at[clip_own], 1, y_peer(k))
    for k in range(1, NZ):
        send(text_in, text_z.at[text_own], 2, z_peer(k))
        send(text_z_ids.at[text_own], text_z_ids.at[text_own], 3, z_peer(k))

    ins = (k_in, q_in, v_in, d_in)

    def send_head(h):
        for a, ref in enumerate(ins):
            mine = aligned(s, tokens)
            pltpu.make_async_copy(
                ref.at[0, :, aligned(s * HEADS_HERE + h, HD)], land.at[h, a, mine], in_local.at[h, a]
            ).start()

            def to_peer(k, carry):
                peer = (k + jnp.where(k >= s, 1, 0), b)
                pltpu.make_async_remote_copy(
                    src_ref=ref.at[0, :, aligned(peer[0] * HEADS_HERE + h, HD)],
                    dst_ref=land.at[h, a, mine],
                    send_sem=in_send.at[h, a], recv_sem=in_recv.at[h, a],
                    device_id=peer, device_id_type=MESH,
                ).start()
                return carry

            lax.fori_loop(0, SEQ - 1, to_peer, 0)

    others = full - tokens

    def wait_sent(h):
        for a in range(4):
            wait_for(land.at[h, a, pl.ds(0, others)], in_send.at[h, a])

    def wait_head(h, a):
        wait_for(land.at[h, a, pl.ds(0, others)], in_recv.at[h, a])
        wait_for(land.at[h, a, pl.ds(0, tokens)], in_local.at[h, a])

    wait_for(clip_y.at[pl.ds(0, 3 * rows)], small_recv.at[0])
    wait_for(clip_y_ids.at[pl.ds(0, 3 * rows)], small_recv.at[1])

    send_head(0)

    group = NY * rows
    clip_load.wait()
    text_load.wait()
    for k in range(1, NX):
        send(clip_y, clip_x.at[aligned(x, group)], 4, x_peer(k))
        send(clip_y_ids, clip_x_ids.at[aligned(x, group)], 5, x_peer(k))
    clip_x[aligned(x, group), :] = clip_y[...]
    clip_x_ids[aligned(x, group), :] = clip_y_ids[...]
    wait_for(text_z.at[pl.ds(0, 3 * rows)], small_recv.at[2])
    wait_for(text_z_ids.at[pl.ds(0, 3 * rows)], small_recv.at[3])
    send(text_z, text_c.at[aligned(c, group)], 6, c_peer)
    send(text_z_ids, text_c_ids.at[aligned(c, group)], 7, c_peer)
    text_c[aligned(c, group), :] = text_z[...]
    text_c_ids[aligned(c, group), :] = text_z_ids[...]

    wait_for(text_c.at[pl.ds(0, group)], small_recv.at[6])
    wait_for(text_c_ids.at[pl.ds(0, group)], small_recv.at[7])
    wait_for(clip_x.at[pl.ds(0, 3 * group)], small_recv.at[4])
    wait_for(clip_x_ids.at[pl.ds(0, 3 * group)], small_recv.at[5])
    scale = scale_ref[0]
    offset = bias_ref[0]
    clip_all = unit_rows(clip_x[...])[0].astype(BF16)
    text_all = unit_rows(text_c[...])[0].astype(BF16)
    logits = scale * nt(clip_all, text_all) + offset
    text_row = jnp.transpose(text_c_ids[...].astype(F32))[0:1, :]
    sign = jnp.where(clip_x_ids[...].astype(F32) == text_row, F32(1.0), F32(-1.0))
    turned = -sign * logits
    small = jnp.exp(-jnp.abs(turned))
    sigmoid = jnp.where(turned >= 0, F32(1.0), small) / (1.0 + small)
    loss_here = jnp.sum(jnp.maximum(turned, 0.0) + jnp.log1p(small))
    pair_grad = (scale * -sign * sigmoid).astype(BF16)
    text_part = tn(pair_grad, clip_all)
    for j in range(NC):
        dc_send[j, 0:group] = text_part[j * group : (j + 1) * group]
        dc_send[j, group : group + 8] = jnp.full((8, text_part.shape[1]), loss_here, F32)
    send(dc_send.at[1 - c], dc_recv, 8, c_peer)
    clip_part = nn(pair_grad, text_all)
    for j in range(NX):
        dx_send[j, 0:group] = clip_part[j * group : (j + 1) * group]
    wait_for(dc_recv, small_recv.at[8])
    text_sum = dc_send[c] + dc_recv[...]
    text_across = across(unit_rows(text_z[...])[0], text_sum[0:group])
    for j in range(NZ):
        dt_own[j] = text_across[j * rows : (j + 1) * rows]
        dt_send[j] = dt_own[j].astype(BF16)
    for j in range(NX):
        dx_send[j, group : group + 8] = text_sum[group : group + 8]
    for k in range(1, NX):
        send(dx_send.at[lax.rem(x + k, NX)], dx_recv.at[x], 9, x_peer(k))
    for k in range(1, NZ):
        send(dt_send.at[lax.rem(z + k, NZ)], dt_recv.at[z], 10, z_peer(k))
    dx_recv[x] = dx_send[x]
    dt_recv[z] = jnp.zeros(dt_recv.shape[1:], BF16)

    wait_sent(0)
    send_head(1)

    def attend(h):
        k_all, q_all, v_all, d_all = (land.at[h, a] for a in range(4))
        for a in range(4):
            wait_head(h, a)
        dk_sum[...] = jnp.zeros_like(dk_sum)
        dv_sum[...] = jnp.zeros_like(dv_sum)

        def step(i, carry):
            r = aligned(i, BLOCK_Q)
            q = q_all[r, :]
            d = d_all[r, :]
            raw_scores = nt(q, k_all[...])
            top = jnp.max(raw_scores, axis=1, keepdims=True)
            expo = jnp.exp2(raw_scores * EXP2_SCALE - top * EXP2_SCALE)
            total = jnp.sum(expo, axis=1, keepdims=True)
            probs = expo * (1.0 / total)
            probs_b = probs.astype(BF16)
            out = nn(probs_b, v_all[...]).astype(BF16)
            res[h, 0, r, :] = out
            dv_sum[...] += tn(probs_b, d)
            dprobs = nt(d, v_all[...])
            delta = jnp.sum(d.astype(F32) * out.astype(F32), axis=1, keepdims=True)
            dscores = (probs * (dprobs - delta)).astype(BF16)
            res[h, 1, r, :] = (nn(dscores, k_all[...]) * INV_ROOT).astype(BF16)
            dk_sum[...] += tn(dscores, q)
            return carry

        lax.fori_loop(0, full // BLOCK_Q, step, 0)
        res[h, 2] = (dk_sum[...] * INV_ROOT).astype(BF16)
        res[h, 3] = dv_sum[...].astype(BF16)

    outs = (o_out, dq_out, dk_out, dv_out)

    def return_head(h):
        for a, ref in enumerate(outs):
            columns = aligned(s * HEADS_HERE + h, HD)
            pltpu.make_async_copy(
                res.at[h, a, aligned(s, tokens)], ref.at[0, :, columns], out_local.at[a]
            ).start()

            def to_peer(k, carry):
                peer = (k + jnp.where(k >= s, 1, 0), b)
                pltpu.make_async_remote_copy(
                    src_ref=res.at[h, a, aligned(peer[0], tokens)],
                    dst_ref=ref.at[0, :, columns],
                    send_sem=out_send.at[a], recv_sem=out_recv.at[a],
                    device_id=peer, device_id_type=MESH,
                ).start()
                return carry

            lax.fori_loop(0, SEQ - 1, to_peer, 0)

    attend(0)
    return_head(0)

    wait_for(dx_recv.at[pl.ds(0, NX - 1)], small_recv.at[9])
    clip_sum = dx_recv[0]
    for j in range(1, NX):
        clip_sum = clip_sum + dx_recv[j]
    clip_across = across(unit_rows(clip_y[...])[0], clip_sum[0:group])
    for j in range(2):
        near_own[j, 0:rows] = clip_across[j * rows : (j + 1) * rows]
        near_own[j, rows : 2 * rows] = clip_across[(2 + j) * rows : (3 + j) * rows]
        near_send[j] = near_own[j].astype(BF16)
    loss_y[0] = clip_sum[group : group + 8, 0:HD]
    send(near_send.at[1 - y_lo], near_recv, 11, y_near)
    send(loss_y.at[0], loss_y.at[1], 13, y_near)

    attend(1)

    wait_for(near_recv, small_recv.at[11])
    wait_for(loss_y.at[0], small_recv.at[13])
    clip_sum = near_own[y_lo] + near_recv[...].astype(F32)
    for j in range(2):
        far_own[j] = clip_sum[j * rows : (j + 1) * rows]
        far_send[j] = far_own[j].astype(BF16)
    loss_recv[s] = loss_y[0] + loss_y[1]
    send(far_send.at[1 - y_hi], far_recv, 14, y_far)
    for k in range(1, SEQ):
        send(loss_recv.at[s], loss_recv.at[s], 12, seq_peer(k))

    return_head(1)

    wait_for(far_recv, small_recv.at[14])
    clip_sum = far_own[y_hi] + far_recv[...].astype(F32)
    grad_clip[...] = raw_grad(clip_y[clip_own, :], clip_sum)

    wait_for(dt_recv.at[pl.ds(0, NZ - 1)], small_recv.at[10])
    text_sum = dt_own[z]
    for j in range(NZ):
        text_sum = text_sum + dt_recv[j].astype(F32)
    grad_text[...] = raw_grad(text_z[text_own, :], text_sum)

    wait_for(loss_recv.at[pl.ds(0, SEQ - 1)], small_recv.at[12])
    loss_sum = loss_recv[0]
    for j in range(1, SEQ):
        loss_sum = loss_sum + loss_recv[j]
    loss_out[...] = loss_sum / (rows * SEQ * BATCH)

    for index, ref in (
        (0, clip_y.at[pl.ds(0, 3 * rows)]),
        (1, clip_y_ids.at[pl.ds(0, 3 * rows)]),
        (2, text_z.at[pl.ds(0, 3 * rows)]),
        (3, text_z_ids.at[pl.ds(0, 3 * rows)]),
        (4, clip_x.at[pl.ds(0, 3 * group)]),
        (5, clip_x_ids.at[pl.ds(0, 3 * group)]),
        (6, text_c.at[pl.ds(0, group)]),
        (7, text_c_ids.at[pl.ds(0, group)]),
        (8, dc_recv),
        (9, dx_recv.at[pl.ds(0, NX - 1)]),
        (10, dt_recv.at[pl.ds(0, NZ - 1)]),
        (11, near_recv),
        (13, loss_y.at[0]),
        (14, far_recv),
        (12, loss_recv.at[pl.ds(0, SEQ - 1)]),
    ):
        wait_for(ref, small_send.at[index])
    wait_sent(1)
    remote = HEADS_HERE * (SEQ - 1) * HD
    for a, ref in enumerate(outs):
        wait_for(ref.at[0, :, pl.ds(0, HEADS_HERE * HD)], out_local.at[a])
        wait_for(ref.at[0, :, pl.ds(0, remote)], out_send.at[a])
        wait_for(ref.at[0, :, pl.ds(0, remote)], out_recv.at[a])


def hand_over(*refs):
    sources, targets, loss, sems = refs[:7], refs[7:14], refs[14], refs[15]
    copies = [pltpu.make_async_copy(sources[a], targets[a], sems.at[a]) for a in range(6)]
    for copy in copies:
        copy.start()
    loss[0] = sources[6][0, 0]
    copies.append(pltpu.make_async_copy(loss, targets[6], sems.at[6]))
    copies[-1].start()
    for copy in copies:
        copy.wait()


def body(queries, key_vectors, value_vectors, cotangent, clip_raw, text_raw, clip_video, text_video, logit_scale, logit_bias):
    tokens = queries.shape[1]
    full = tokens * SEQ
    rows, width = clip_raw.shape
    in_hbm = pl.BlockSpec(memory_space=pl.ANY)
    in_vmem = pl.BlockSpec(memory_space=pltpu.VMEM)
    in_smem = pl.BlockSpec(memory_space=pltpu.SMEM)
    group = NY * rows
    dma = pltpu.SemaphoreType.DMA
    in_place = (queries, key_vectors, value_vectors, cotangent, clip_raw, text_raw, clip_video, text_video)
    results = pl.pallas_call(
        kernel,
        out_shape=(
            *[pltpu.VMEM(queries.shape, BF16)] * 4,
            pltpu.VMEM((rows, width), F32),
            pltpu.VMEM((rows, width), F32),
            pltpu.VMEM((8, HD), F32),
        ),
        in_specs=[in_hbm] * 8 + [in_smem] * 2,
        out_specs=[in_vmem] * 7,
        scratch_shapes=[
            pltpu.SMEM((rows,), jnp.int32),
            pltpu.SMEM((rows,), jnp.int32),
            dma((4,)),
            pltpu.VMEM((HEADS_HERE, 4, full, HD), BF16),
            pltpu.VMEM((HEADS_HERE, 4, full, HD), BF16),
            pltpu.VMEM((full, HD), F32),
            pltpu.VMEM((full, HD), F32),
            pltpu.VMEM((group, width), BF16),
            pltpu.VMEM((group, HD), jnp.int32),
            pltpu.VMEM((NX * group, width), BF16),
            pltpu.VMEM((NX * group, HD), jnp.int32),
            pltpu.VMEM((NZ * rows, width), BF16),
            pltpu.VMEM((NZ * rows, HD), jnp.int32),
            pltpu.VMEM((NC * NZ * rows, width), BF16),
            pltpu.VMEM((NC * NZ * rows, HD), jnp.int32),
            pltpu.VMEM((NC, group + 8, width), F32),
            pltpu.VMEM((group + 8, width), F32),
            pltpu.VMEM((NX, group + 8, width), F32),
            pltpu.VMEM((NX, group + 8, width), F32),
            pltpu.VMEM((2, 2 * rows, width), F32),
            pltpu.VMEM((2, 2 * rows, width), BF16),
            pltpu.VMEM((2 * rows, width), BF16),
            pltpu.VMEM((2, rows, width), F32),
            pltpu.VMEM((2, rows, width), BF16),
            pltpu.VMEM((rows, width), BF16),
            pltpu.VMEM((2, 8, HD), F32),
            pltpu.VMEM((NZ, rows, width), F32),
            pltpu.VMEM((NZ, rows, width), BF16),
            pltpu.VMEM((NZ, rows, width), BF16),
            pltpu.VMEM((SEQ, 8, HD), F32),
            dma((HEADS_HERE, 4)),
            dma((HEADS_HERE, 4)),
            dma((HEADS_HERE, 4)),
            dma((4,)),
            dma((4,)),
            dma((4,)),
            dma((15,)),
            dma((15,)),
        ],
        compiler_params=pltpu.CompilerParams(
            collective_id=0, has_side_effects=True, vmem_limit_bytes=48 * 2**20
        ),
        cost_estimate=pl.CostEstimate(
            flops=HEADS_HERE * 12 * full * full * HD, bytes_accessed=8 * full * HD * 2, transcendentals=HEADS_HERE * full * full
        ),
        name="tower",
    )(*[pltpu.with_memory_space_constraint(array, pltpu.HBM) for array in in_place], logit_scale, logit_bias)
    return pl.pallas_call(
        hand_over,
        out_shape=(
            *[jax.ShapeDtypeStruct(queries.shape, BF16)] * 4,
            jax.ShapeDtypeStruct((rows, width), F32),
            jax.ShapeDtypeStruct((rows, width), F32),
            jax.ShapeDtypeStruct((1,), F32),
        ),
        in_specs=[in_vmem] * 7,
        out_specs=[in_hbm] * 7,
        scratch_shapes=[pltpu.SMEM((1,), F32), dma((7,))],
        name="hand_over",
    )(*[pltpu.with_memory_space_constraint(array, pltpu.VMEM) for array in results])


def solution(mesh):
    tokens = P("batch", "seq", None)
    embeddings = P(("seq", "batch"), None)
    ids = P(("seq", "batch"))
    return jax.shard_map(
        body,
        mesh=mesh,
        in_specs=(tokens,) * 4 + (embeddings,) * 2 + (ids,) * 2 + (P(), P()),
        out_specs=(tokens,) * 4 + (embeddings,) * 2 + (P(),),
        check_vma=False,
    )
```
